128 devices in a mesh: rep: 16 (over x, y_lo, core), grp: 8 (over y_hi, z).
Axes of the slice: x: 4, y: 4 (y_hi: 2, y_lo: 2; y = y_hi * 2 + y_lo), z: 4, core: 2. Of those that a mesh axis runs over, the one named last changes fastest.
Arguments:
- tokens: bfloat16 [16, 1536, 1024], P('rep', 'grp'), may hold values from -6 to 6
- span_order: int32 [16, 16], P('rep'), may hold values from 0 to 15, each once within a row
- query_weight: bfloat16 [1024, 1024], P('grp'), may hold values from -0.1875 to 0.1875
- key_weight: bfloat16 [1024, 512], P('grp'), may hold values from -0.1875 to 0.1875
- value_weight: bfloat16 [1024, 512], P('grp'), may hold values from -0.1875 to 0.1875
- out_weight: bfloat16 [1024, 1024], P('grp'), may hold values from -1.5 to 1.5
- gate_weight: bfloat16 [1024, 4608], P('grp'), may hold values from -0.1875 to 0.1875
- up_weight: bfloat16 [1024, 4608], P('grp'), may hold values from -0.1875 to 0.1875
- down_weight: bfloat16 [4608, 1024], P('grp'), may hold values from -0.09375 to 0.09375
- attn_gain: bfloat16 [1024], P('grp'), may hold values from 0.25 to 1.75
- ffn_gain: bfloat16 [1024], P('grp'), may hold values from 0.25 to 1.75
- query_gain: bfloat16 [64], P('grp'), may hold values from 0.25 to 1.75
- key_gain: bfloat16 [64], P('grp'), may hold values from 0.25 to 1.75
- cotangent: bfloat16 [16, 1536, 1024], P('rep', 'grp'), may hold values from -6 to 6
Outputs:
- outputs: bfloat16 [16, 1536, 1024], P('rep', 'grp')
- input_grad: float32 [16, 1536, 1024], P('rep', 'grp')
- query_grad: float32 [1024, 1024], P('grp')
- key_grad: float32 [1024, 512], P('grp')
- value_grad: float32 [1024, 512], P('grp')
- out_grad: float32 [1024, 1024], P('grp')
- gate_grad: float32 [1024, 4608], P('grp')
- up_grad: float32 [1024, 4608], P('grp')
- down_grad: float32 [4608, 1024], P('grp')
- attn_gain_grad: float32 [1024], P('grp')
- ffn_gain_grad: float32 [1024], P('grp')
- query_gain_grad: float32 [64], P('grp')
- key_gain_grad: float32 [64], P('grp')
The draws below stay inside these ranges and needn't reach their ends.
Inputs may be any that keep to these rules, and one draw needn't show every extreme that they name: `span_order`: each row is a permutation: the stored blocks of a sequence hold all 16 blocks of positions once each.
All inputs are finite; a program needn't handle non-finite values.
Results may differ from the reference program's by a relative error of at most 0.034.
Values may be sent and summed in bfloat16 or wider, within the bound.
No kernel may reach another device: no remote copies, remote signals or barrier semaphores. Data moves between devices by JAX's collectives and lax.ppermute only.
A program may use at most 192 MiB of HBM per device.

```python
import math
import jax
import jax.numpy as jnp
from jax import lax

D = 1024
FF = 4608
H = 16
KVH = 8
HD = 64
CH = 96
SEQ = 1536
SEQS = 16
SPANS = 16


def block_levels(key, shape, shards, smallest, top_value):
    def one(dim, blocks):
        draws = jax.random.uniform(jax.random.fold_in(jax.random.fold_in(key, 6), dim), (blocks,), jnp.float32, smallest / len(shards), top_value / len(shards))
        return jnp.repeat(jnp.exp(draws), shape[dim] // blocks).reshape((-1,) + (1,) * (len(shape) - dim - 1))

    level = one(*shards[0])
    for cut in shards[1:]:
        level = level * one(*cut)
    return level


def scatter_about(key, dims, deviation, most, shards=(), kind=jnp.bfloat16):
    drawn = deviation * jax.random.normal(key, dims, jnp.float32)
    if shards:
        drawn = drawn * block_levels(key, dims, shards, -0.22, 0.18)
    return jnp.clip(drawn, -most, most).astype(kind)


def setup_inputs(seed: int = 0) -> dict:
    splits = jax.random.split(jax.random.key(seed), 15)
    tokens = scatter_about(splits[0], (SEQS, SEQ, D), 1.0, 6.0, ((0, 16), (1, 8)))
    span_order = jax.vmap(lambda own: jax.random.permutation(own, SPANS))(jax.random.split(splits[1], SEQS)).reshape((SEQS, SPANS)).astype(jnp.int32)
    query_weight = scatter_about(splits[2], (D, H * HD), D ** -0.5, 0.1875, ((0, 8),))
    key_weight = scatter_about(splits[3], (D, KVH * HD), D ** -0.5, 0.1875, ((0, 8),))
    value_weight = scatter_about(splits[4], (D, KVH * HD), D ** -0.5, 0.1875, ((0, 8),))
    out_weight = scatter_about(splits[5], (H * HD, D), (max(1, H * HD // 64)) ** -0.5, 1.5, ((0, 8),))
    gate_weight = scatter_about(splits[6], (D, FF), D ** -0.5, 0.1875, ((0, 8),))
    up_weight = scatter_about(splits[7], (D, FF), D ** -0.5, 0.1875, ((0, 8),))
    down_weight = scatter_about(splits[8], (FF, D), FF ** -0.5, 0.09375, ((0, 8),))
    attn_gain = jnp.clip(1.0 + 0.15 * jax.random.normal(splits[9], (D,), jnp.float32), 0.25, 1.75).astype(jnp.bfloat16)
    ffn_gain = jnp.clip(1.0 + 0.15 * jax.random.normal(splits[10], (D,), jnp.float32), 0.25, 1.75).astype(jnp.bfloat16)
    query_gain = jnp.clip(1.0 + 0.15 * jax.random.normal(splits[11], (HD,), jnp.float32), 0.25, 1.75).astype(jnp.bfloat16)
    key_gain = jnp.clip(1.0 + 0.15 * jax.random.normal(splits[12], (HD,), jnp.float32), 0.25, 1.75).astype(jnp.bfloat16)
    cotangent = scatter_about(splits[13], (SEQS, SEQ, D), 1.0, 6.0, ((0, 16), (1, 8)))
    return dict(tokens=tokens, span_order=span_order, query_weight=query_weight, key_weight=key_weight, value_weight=value_weight, out_weight=out_weight, gate_weight=gate_weight, up_weight=up_weight, down_weight=down_weight, attn_gain=attn_gain, ffn_gain=ffn_gain, query_gain=query_gain, key_gain=key_gain, cotangent=cotangent)


@jax.custom_vjp
def low(v):
    return lax.optimization_barrier(v.astype(jnp.bfloat16)).astype(jnp.float32)

@jax.custom_vjp
def low_back(v):
    return v

def low_keep(v):
    return (low(v), None)

def low_pass(kept, grad):
    return (grad,)

def back_keep(v):
    return (v, None)

def back_low(kept, grad):
    return (low(grad),)
low.defvjp(low_keep, low_pass)
low_back.defvjp(back_keep, back_low)
epsilon = 1e-05
theta_base = 1000000.0
masked_score = -1e+30
highest = lax.Precision.HIGHEST

def rms_norm(values, gain):
    return values * lax.rsqrt(lax.optimization_barrier(jnp.mean(values * values, axis=-1, keepdims=True)) + epsilon) * gain

def rotary(positions):
    half = HD // 2
    ladder = jnp.arange(half, dtype=jnp.float32) * (2.0 / HD)
    freq = jnp.exp(-math.log(theta_base) * ladder)
    angle = positions.astype(jnp.float32)[:, None] * freq[None, :]
    both = jnp.concatenate([angle, angle], axis=1)
    return (jnp.cos(both), jnp.sin(both))

def turn(values, cosine, sine):
    half = values.shape[-1] // 2
    rotated = jnp.concatenate([-values[..., half:], values[..., :half]], axis=-1)
    return values * cosine[:, None, :] + rotated * sine[:, None, :]

def place_rows(order_row):
    index = jnp.arange(SEQ, dtype=jnp.int32)
    return order_row[index // CH].astype(jnp.int32) * CH + index % CH

def layer(x_in, positions, params):
    query_weight, key_weight, value_weight, out_weight, gate_weight, up_weight, down_weight, attn_gain, ffn_gain, query_gain, key_gain = params
    cosine, sine = rotary(positions)
    input_attn = low(rms_norm(x_in, attn_gain))
    query_lin = low_back(jnp.dot(input_attn, query_weight, precision=highest))
    key_lin = low_back(jnp.dot(input_attn, key_weight, precision=highest))
    values = low_back(low(jnp.dot(input_attn, value_weight, precision=highest)))
    queries = low(turn(rms_norm(query_lin.reshape(SEQ, H, HD), query_gain), cosine, sine))
    keys = low(turn(rms_norm(key_lin.reshape(SEQ, KVH, HD), key_gain), cosine, sine))
    keys_wide = jnp.repeat(keys, H // KVH, axis=1)
    values_wide = jnp.repeat(values.reshape(SEQ, KVH, HD), H // KVH, axis=1)
    blocks = queries.reshape(SPANS, CH, H, HD)
    block_pos = positions.reshape(SPANS, CH)

    def attend_block(items):
        query_block, pos_block = items
        scores = jnp.einsum('qhd,khd->hqk', query_block, keys_wide, precision=highest) * HD ** (-0.5)
        scores = low_back(scores)
        visible = pos_block[:, None] >= positions[None, :]
        scores = jnp.where(visible[None], scores, masked_score)
        attend = low(jax.nn.softmax(scores, axis=-1))
        return jnp.einsum('hqk,khd->qhd', attend, values_wide, precision=highest)
    mixed = lax.map(jax.checkpoint(attend_block), (blocks, block_pos)).reshape(SEQ, H * HD)
    mixed = low_back(low(mixed))
    mid = x_in + low_back(jnp.dot(mixed, out_weight, precision=highest))
    input_ffn = low(rms_norm(mid, ffn_gain))
    gate = low_back(jnp.dot(input_ffn, gate_weight, precision=highest))
    up = low_back(jnp.dot(input_ffn, up_weight, precision=highest))
    hidden = low(jax.nn.silu(gate) * up)
    return mid + jnp.dot(hidden, down_weight, precision=highest)

def reference(tokens, span_order, query_weight, key_weight, value_weight, out_weight, gate_weight, up_weight, down_weight, attn_gain, ffn_gain, query_gain, key_gain, cotangent):
    params = tuple((p.astype(jnp.float32) for p in (query_weight, key_weight, value_weight, out_weight, gate_weight, up_weight, down_weight, attn_gain, ffn_gain, query_gain, key_gain)))

    def one_sequence(totals, item):
        seq_tokens, seq_order, seq_cot = item
        positions = place_rows(seq_order)

        def run(x_in, *weights):
            return layer(x_in, positions, weights)
        result, pull = jax.vjp(run, seq_tokens.astype(jnp.float32), *params)
        grads = pull(seq_cot.astype(jnp.float32))
        totals = tuple((t + g for t, g in zip(totals, grads[1:])))
        return (totals, (result.astype(jnp.bfloat16), grads[0]))
    start = tuple((jnp.zeros(p.shape, jnp.float32) for p in params))
    totals, (outputs, input_grad) = lax.scan(one_sequence, start, (tokens, span_order, cotangent))
    return (outputs, input_grad, totals[0], totals[1], totals[2], totals[3], totals[4], totals[5], totals[6], totals[7], totals[8], totals[9], totals[10])
```

```python
import functools
import math

import jax
import jax.numpy as jnp
from jax import lax
from jax.experimental import pallas as pl
from jax.experimental.pallas import tpu as pltpu
from jax.sharding import PartitionSpec as P

H = 16
KVH = 8
HD = 64
CH = 96
SEQ = 1536
SPANS = 16
TILE = 256
EPS = 1e-05
THETA = 1000000.0
AXES = ("rep", "grp")
F32 = jnp.float32
BF16 = jnp.bfloat16
VMEM_LIMIT = 48 * 1024 * 1024


def coords(i):
    rep, grp = divmod(i, 8)
    return rep // 4, (rep // 2) % 2, rep % 2, grp // 4, grp % 4


def index_of(x, ylo, core, yhi, z):
    return ((x * 2 + ylo) * 2 + core) * 8 + yhi * 4 + z


def permutation(move):
    return [(i, index_of(*move(*coords(i)))) for i in range(128)]


X_UP = permutation(lambda x, a, c, b, z: ((x + 1) % 4, a, c, b, z))
X_DOWN = permutation(lambda x, a, c, b, z: ((x - 1) % 4, a, c, b, z))
Y_SWAP = permutation(lambda x, a, c, b, z: (x, 1 - a, c, b, z))
CORE_SWAP = permutation(lambda x, a, c, b, z: (x, a, 1 - c, b, z))


def send(value, perm):
    return lax.ppermute(value, AXES, perm)


def exchange_grp(value):
    return lax.all_to_all(value, "grp", 0, 0)


def gather_grp(piece):
    return exchange_grp(jnp.broadcast_to(piece[None], (8,) + piece.shape))


def x_gather(own):
    half = own.shape[0] // 2
    left = send(own, X_UP)
    right = send(own, X_DOWN)
    far_a = send(left[:half], X_UP)
    far_b = send(right[half:], X_DOWN)
    return own, left, right, jnp.concatenate([far_a, far_b], axis=0)


def x_reduce(parts):
    own, left, right, far = parts
    half = own.shape[0] // 2
    far = far.astype(BF16)
    got_a = send(far[:half], X_UP)
    got_b = send(far[half:], X_DOWN)
    right = jnp.concatenate([right[:half] + got_a.astype(F32), right[half:]], axis=0)
    left = jnp.concatenate([left[:half], left[half:] + got_b.astype(F32)], axis=0)
    from_left = send(right.astype(BF16), X_UP)
    from_right = send(left.astype(BF16), X_DOWN)
    return own + from_left.astype(F32) + from_right.astype(F32)


def rms_norm(values, gain):
    return values * lax.rsqrt(jnp.mean(values * values, axis=-1, keepdims=True) + EPS) * gain


def rotary(positions):
    half = HD // 2
    ladder = jnp.arange(half, dtype=F32) * (2.0 / HD)
    freq = jnp.exp(-math.log(THETA) * ladder)
    angle = positions.astype(F32)[:, None] * freq[None, :]
    both = jnp.concatenate([angle, angle], axis=1)
    return jnp.cos(both), jnp.sin(both)


def turn(values, cosine, sine):
    half = HD // 2
    rotated = jnp.concatenate([-values[..., half:], values[..., :half]], axis=-1)
    return values * cosine[:, None, None, :] + rotated * sine[:, None, None, :]


def mask_tile():
    key = lax.broadcasted_iota(jnp.int32, (TILE, 2 * TILE), 0)
    query = lax.broadcasted_iota(jnp.int32, (TILE, 2 * TILE), 1)
    return key <= jnp.where(query >= TILE, query - TILE, query)


def dot(a, b):
    return jnp.dot(a, b, preferred_element_type=F32)


def sort_rows(order_ref, source, target):
    for c in range(SPANS):
        start = pl.multiple_of(order_ref[c] * CH, CH)
        target[pl.ds(start, CH), :] = source[c * CH : (c + 1) * CH, :]


def forward_kernel(order_ref, qkv_ref, mixed_ref, out_t_ref, log_ref, rows, cols, keys):
    sort_rows(order_ref, qkv_ref, rows)
    tiles = SEQ // TILE
    for i in range(tiles):
        span = slice(i * TILE, (i + 1) * TILE)
        cols[:, span] = rows[span, :].astype(F32).T.astype(BF16)
        keys[span, :] = rows[span, 128:192]
    mask = mask_tile()
    for i in range(tiles):
        span = slice(i * TILE, (i + 1) * TILE)
        query = jnp.concatenate([cols[0:64, span], cols[64:128, span]], axis=1)
        query = (query.astype(F32) * HD ** (-0.5)).astype(BF16)
        total = jnp.zeros((64, 2 * TILE), F32)
        weight = jnp.zeros((1, 2 * TILE), F32)
        for c in range(i + 1):
            key_span = slice(c * TILE, (c + 1) * TILE)
            expo = jnp.exp(dot(keys[key_span, :], query))
            if c == i:
                expo = jnp.where(mask, expo, 0.0)
            weight = weight + jnp.sum(expo, axis=0, keepdims=True)
            total = total + dot(cols[192:256, key_span], expo.astype(BF16))
        total = total / weight
        logs = jnp.log(weight)
        out_t_ref[0:64, span] = total[:, :TILE]
        out_t_ref[64:128, span] = total[:, TILE:]
        log_ref[0:1, span] = logs[:, :TILE]
        log_ref[1:2, span] = logs[:, TILE:]
    log_ref[2:8, :] = jnp.zeros((6, SEQ), F32)
    for i in range(tiles):
        span = slice(i * TILE, (i + 1) * TILE)
        rows[span, 0:128] = out_t_ref[:, span].T.astype(BF16)
    for c in range(SPANS):
        start = pl.multiple_of(order_ref[c] * CH, CH)
        mixed_ref[c * CH : (c + 1) * CH, :] = rows[pl.ds(start, CH), 0:128]


def attend_forward(order, qkv):
    return pl.pallas_call(
        forward_kernel,
        out_shape=(
            jax.ShapeDtypeStruct((SEQ, 128), BF16),
            jax.ShapeDtypeStruct((128, SEQ), F32),
            jax.ShapeDtypeStruct((8, SEQ), F32),
        ),
        in_specs=[
            pl.BlockSpec(memory_space=pltpu.SMEM),
            pl.BlockSpec(memory_space=pltpu.VMEM),
        ],
        out_specs=(pl.BlockSpec(memory_space=pltpu.VMEM),) * 3,
        scratch_shapes=[
            pltpu.VMEM((SEQ, 256), BF16),
            pltpu.VMEM((256, SEQ), BF16),
            pltpu.VMEM((SEQ, 64), BF16),
        ],
        compiler_params=pltpu.CompilerParams(vmem_limit_bytes=VMEM_LIMIT),
        cost_estimate=pl.CostEstimate(
            flops=4 * 10**9, bytes_accessed=3 * 10**6, transcendentals=3 * 10**6
        ),
        name="attend_forward",
    )(order, qkv)


def backward_kernel(
    order_ref, qkv_ref, grad_ref, out_t_ref, log_ref, result_ref,
    rows, cols, grad_rows, grad_cols, keys, values, grad_keys, grad_values, grad_query,
):
    sort_rows(order_ref, qkv_ref, rows)
    sort_rows(order_ref, grad_ref, grad_rows)
    tiles = SEQ // TILE
    for i in range(tiles):
        span = slice(i * TILE, (i + 1) * TILE)
        cols[:, span] = rows[span, :].astype(F32).T.astype(BF16)
        grad_cols[:, span] = grad_rows[span, :].astype(F32).T.astype(BF16)
        keys[span, :] = rows[span, 128:192]
        values[span, :] = rows[span, 192:256]
    grad_keys[...] = jnp.zeros_like(grad_keys)
    grad_values[...] = jnp.zeros_like(grad_values)
    mask = mask_tile()
    scale = HD ** (-0.5)
    for i in range(tiles):
        span = slice(i * TILE, (i + 1) * TILE)
        query = jnp.concatenate([cols[0:64, span], cols[64:128, span]], axis=1)
        query = (query.astype(F32) * scale).astype(BF16)
        grad = jnp.concatenate([grad_cols[0:64, span], grad_cols[64:128, span]], axis=1)
        query_rows = jnp.concatenate([rows[span, 0:64], rows[span, 64:128]], axis=0)
        query_rows = (query_rows.astype(F32) * scale).astype(BF16)
        grad_tile = jnp.concatenate([grad_rows[span, 0:64], grad_rows[span, 64:128]], axis=0)
        logs = jnp.concatenate([log_ref[0:1, span], log_ref[1:2, span]], axis=1)
        out_t = jnp.concatenate([out_t_ref[0:64, span], out_t_ref[64:128, span]], axis=1)
        inner = jnp.sum(out_t * grad.astype(F32), axis=0, keepdims=True)
        total = jnp.zeros((64, 2 * TILE), F32)
        for c in range(i + 1):
            key_span = slice(c * TILE, (c + 1) * TILE)
            attend = jnp.exp(dot(keys[key_span, :], query) - logs)
            if c == i:
                attend = jnp.where(mask, attend, 0.0)
            grad_values[key_span, :] += dot(attend.astype(BF16), grad_tile)
            grad_attend = dot(values[key_span, :], grad)
            grad_scores = (attend * (grad_attend - inner)).astype(BF16)
            grad_keys[key_span, :] += dot(grad_scores, query_rows)
            total = total + dot(cols[128:192, key_span], grad_scores)
        total = total * scale
        grad_query[0:64, span] = total[:, :TILE]
        grad_query[64:128, span] = total[:, TILE:]
    for i in range(tiles):
        span = slice(i * TILE, (i + 1) * TILE)
        rows[span, 0:128] = grad_query[:, span].T.astype(BF16)
        rows[span, 128:256] = jnp.concatenate(
            [grad_keys[span, :], grad_values[span, :]], axis=1
        ).astype(BF16)
    for c in range(SPANS):
        start = pl.multiple_of(order_ref[c] * CH, CH)
        result_ref[c * CH : (c + 1) * CH, :] = rows[pl.ds(start, CH), :]


def attend_backward(order, qkv, grad, out_t, logs):
    return pl.pallas_call(
        backward_kernel,
        out_shape=jax.ShapeDtypeStruct((SEQ, 256), BF16),
        in_specs=[pl.BlockSpec(memory_space=pltpu.SMEM)]
        + [pl.BlockSpec(memory_space=pltpu.VMEM)] * 4,
        out_specs=pl.BlockSpec(memory_space=pltpu.VMEM),
        scratch_shapes=[
            pltpu.VMEM((SEQ, 256), BF16),
            pltpu.VMEM((256, SEQ), BF16),
            pltpu.VMEM((SEQ, 128), BF16),
            pltpu.VMEM((128, SEQ), BF16),
            pltpu.VMEM((SEQ, 64), BF16),
            pltpu.VMEM((SEQ, 64), BF16),
            pltpu.VMEM((SEQ, 64), F32),
            pltpu.VMEM((SEQ, 64), F32),
            pltpu.VMEM((128, SEQ), F32),
        ],
        compiler_params=pltpu.CompilerParams(vmem_limit_bytes=VMEM_LIMIT),
        cost_estimate=pl.CostEstimate(
            flops=10 * 10**9, bytes_accessed=4 * 10**6, transcendentals=3 * 10**6
        ),
        name="attend_backward",
    )(order, qkv, grad, out_t, logs)


def swiglu(gate_in, up_in):
    return jax.nn.silu(gate_in) * up_in


def per_device(
    tokens, span_order, query_weight, key_weight, value_weight, out_weight,
    gate_weight, up_weight, down_weight, attn_gain, ffn_gain, query_gain, key_gain, cotangent,
):
    rep = lax.axis_index("rep")
    place = lax.axis_index("grp")
    xpos, core = rep // 4, rep % 2
    rows = tokens.shape[1]
    order_row = span_order[0]

    def core_half(matrix):
        half = matrix.shape[0] // 2
        return lax.dynamic_slice_in_dim(matrix, core * half, half, 0)

    def both_cores(mine):
        other = send(mine, CORE_SWAP)
        first = jnp.where(core == 0, mine, other)
        second = jnp.where(core == 0, other, mine)
        return jnp.stack([first, second], axis=1).reshape(-1, mine.shape[-1])

    grouped = jnp.concatenate(
        [
            query_weight.reshape(128, KVH, 128),
            key_weight.reshape(128, KVH, HD),
            value_weight.reshape(128, KVH, HD),
        ],
        axis=2,
    ).reshape(128, 2048)
    extra = jnp.concatenate(
        [
            attn_gain[:, None],
            ffn_gain[:, None],
            jnp.broadcast_to(query_gain[None], (128, 8)),
            jnp.broadcast_to(key_gain[None], (128, 8)),
            jnp.zeros((128, 110), BF16),
        ],
        axis=1,
    )
    wide = both_cores(gather_grp(core_half(jnp.concatenate([grouped, extra], axis=1))))
    qkv_full = wide[:, :2048]
    gains = wide[:, 2048:].astype(F32)
    attn_scale = gains[:, 0]
    ffn_scale = gains[:, 1]
    query_scale = gains[::128, 2:10].reshape(HD)
    key_scale = gains[::128, 10:18].reshape(HD)

    def x_columns(matrix):
        cut = matrix.reshape(128, 8, 4, 144)
        return lax.dynamic_index_in_dim(cut, xpos, 2, keepdims=False).reshape(128, 1152)

    gate_up_piece = core_half(jnp.concatenate([x_columns(gate_weight), x_columns(up_weight)], axis=1))
    down_piece = core_half(
        lax.dynamic_index_in_dim(down_weight.reshape(4, 144, 1024), xpos, 0, keepdims=False)
    )
    gate_up_half = lax.all_gather(gate_up_piece, "grp", axis=0, tiled=False)
    down_half = lax.all_gather(down_piece, "grp", axis=0, tiled=False)
    out_full = both_cores(gather_grp(core_half(out_weight)))

    cot = jnp.concatenate(x_gather(cotangent[0]), axis=0)

    x_in = tokens[0].astype(F32)
    blocks = lax.dynamic_slice_in_dim(order_row, place * 2, 2, 0)
    positions = (blocks[:, None] * CH + jnp.arange(CH, dtype=jnp.int32)[None, :]).reshape(rows)
    cosine, sine = rotary(positions)
    head_scale = jnp.stack([query_scale, query_scale, key_scale])

    def shape_heads(lin, gain):
        return turn(rms_norm(lin, gain[None, None]), cosine, sine)

    input_attn = rms_norm(x_in, attn_scale).astype(BF16)
    lin = dot(input_attn, qkv_full).reshape(rows, KVH, 4, HD)
    shaped_lin = lin[:, :, :3]
    shaped = shape_heads(shaped_lin, head_scale)
    packed = jnp.concatenate([shaped, lin[:, :, 3:]], axis=2).astype(BF16)
    packed = packed.reshape(rows, KVH, 256).transpose(1, 0, 2)
    qkv = exchange_grp(packed).reshape(SEQ, 256)
    mixed_heads, out_t, logs = attend_forward(order_row, qkv)
    mixed = exchange_grp(mixed_heads.reshape(8, rows, 128)).transpose(1, 0, 2).reshape(rows, 1024)
    x_mid = x_in + dot(mixed, out_full)

    input_ffn_own = rms_norm(x_mid, ffn_scale).astype(BF16)
    input_ffn = jnp.concatenate(x_gather(input_ffn_own), axis=0)
    gate_up_full = both_cores(gate_up_half)
    down_full = both_cores(down_half)
    gate_up = dot(input_ffn, gate_up_full)
    gate, up_value = gate_up[:, :1152], gate_up[:, 1152:]
    hidden_exact, pull_swiglu = jax.vjp(swiglu, gate, up_value)
    hidden = hidden_exact.astype(BF16)
    grad_hidden = jnp.einsum("td,fd->tf", cot, down_full, preferred_element_type=F32)
    grad_gate, grad_up = pull_swiglu(grad_hidden)
    grad_gate_up = jnp.concatenate([grad_gate.astype(BF16), grad_up.astype(BF16)], axis=1)
    grad_input_part = jnp.einsum(
        "tf,df->td", grad_gate_up, gate_up_full, preferred_element_type=F32
    )
    grad_input_ffn = x_reduce(grad_input_part.reshape(4, rows, 1024))
    down_part = dot(hidden, down_full)
    outputs = (x_mid + x_reduce(down_part.reshape(4, rows, 1024))).astype(BF16)[None]

    def core_sum(full, half):
        low = full.astype(BF16).reshape(8, 2, half, full.shape[-1])
        mine = lax.dynamic_index_in_dim(low, core, 1, keepdims=False)
        theirs = lax.dynamic_index_in_dim(low, 1 - core, 1, keepdims=False)
        return (mine.astype(F32) + send(theirs, CORE_SWAP).astype(F32)).astype(BF16)

    def y_sum(value):
        return (value.astype(F32) + send(value, Y_SWAP).astype(F32)).astype(BF16)

    def x_sum(value):
        own, left, right, far = x_gather(value)
        return (own.astype(F32) + far.astype(F32)) + (left.astype(F32) + right.astype(F32))

    gate_up_grad = jnp.einsum("td,tf->df", input_ffn, grad_gate_up, preferred_element_type=F32)
    down_grad = jnp.einsum("tf,td->fd", hidden, cot, preferred_element_type=F32)
    gate_up_sum = y_sum(
        lax.psum_scatter(core_sum(gate_up_grad, 64), "grp", scatter_dimension=0, tiled=False)
    )
    down_sum = y_sum(
        lax.psum_scatter(core_sum(down_grad, 72), "grp", scatter_dimension=0, tiled=False)
    )

    _, pull_ffn_norm = jax.vjp(rms_norm, x_mid, ffn_scale)
    grad_mid_norm, ffn_gain_grad = pull_ffn_norm(grad_input_ffn)
    grad_mid = cotangent[0].astype(F32) + grad_mid_norm
    grad_attn = grad_mid.astype(BF16)
    grad_mixed = jnp.einsum(
        "td,fd->tf", grad_attn, out_full, preferred_element_type=F32
    ).astype(BF16)
    out_grad = jnp.einsum("tf,td->fd", mixed, grad_attn, preferred_element_type=F32)
    grad_heads = exchange_grp(grad_mixed.reshape(rows, 8, 128).transpose(1, 0, 2))
    grad_qkv = attend_backward(order_row, qkv, grad_heads.reshape(SEQ, 128), out_t, logs)
    grad_packed = exchange_grp(grad_qkv.reshape(8, rows, 256)).transpose(1, 0, 2)
    grad_packed = grad_packed.reshape(rows, KVH, 4, HD)

    _, pull_heads = jax.vjp(shape_heads, shaped_lin, head_scale)
    grad_shaped, head_gain_grad = pull_heads(grad_packed[:, :, :3].astype(F32))
    grad_lin = jnp.concatenate([grad_shaped.astype(BF16), grad_packed[:, :, 3:]], axis=2)
    grad_lin = grad_lin.reshape(rows, 2048)
    grad_input_attn = jnp.einsum("tf,df->td", grad_lin, qkv_full, preferred_element_type=F32)
    qkv_grad = jnp.einsum("td,tf->df", input_attn, grad_lin, preferred_element_type=F32)
    _, pull_attn_norm = jax.vjp(rms_norm, x_in, attn_scale)
    grad_in_norm, attn_gain_grad = pull_attn_norm(grad_input_attn)
    input_grad = (grad_mid + grad_in_norm)[None]

    query_gain_grad = head_gain_grad[0] + head_gain_grad[1]
    key_gain_grad = head_gain_grad[2]
    extra_grad = jnp.concatenate(
        [
            attn_gain_grad[:, None],
            ffn_gain_grad[:, None],
            jnp.repeat(query_gain_grad.reshape(8, 8), 128, axis=0),
            jnp.repeat(key_gain_grad.reshape(8, 8), 128, axis=0),
            jnp.zeros((1024, 110), F32),
        ],
        axis=1,
    )
    wide_grad = jnp.concatenate([qkv_grad, extra_grad], axis=1)
    out_sum = x_sum(
        y_sum(
            jnp.sum(exchange_grp(core_sum(out_grad, 64)).astype(F32), axis=0).astype(BF16)
        )
    )
    wide_sum = x_sum(
        y_sum(
            jnp.sum(exchange_grp(core_sum(wide_grad, 64)).astype(F32), axis=0).astype(BF16)
        )
    )

    def pair(value):
        other = send(value, CORE_SWAP)
        return jnp.where(
            core == 0,
            jnp.concatenate([value, other], axis=0),
            jnp.concatenate([other, value], axis=0),
        )

    def x_order(value):
        parts = x_gather(value)
        result = jnp.zeros((4,) + value.shape, value.dtype)
        for part, offset in zip(parts, (0, 3, 1, 2)):
            result = lax.dynamic_update_slice(
                result, part[None], ((xpos + offset) % 4, 0, 0)
            )
        return result

    gate_up_all = x_order(pair(gate_up_sum)).reshape(4, 128, 2, 8, 144)
    gate_up_all = gate_up_all.transpose(2, 1, 3, 0, 4).reshape(2, 128, 4608).astype(F32)
    down_all = x_order(pair(down_sum)).reshape(576, 1024).astype(F32)
    out_all = pair(out_sum.astype(BF16)).astype(F32)
    wide_all = pair(wide_sum.astype(BF16)).astype(F32)
    grouped_all = wide_all[:, :2048].reshape(128, KVH, 256)
    extra_all = wide_all[:, 2048:]
    return (
        outputs,
        input_grad,
        grouped_all[:, :, :128].reshape(128, 1024),
        grouped_all[:, :, 128:192].reshape(128, 512),
        grouped_all[:, :, 192:].reshape(128, 512),
        out_all,
        gate_up_all[0],
        gate_up_all[1],
        down_all,
        extra_all[:, 0],
        extra_all[:, 1],
        extra_all[0, 2:10],
        extra_all[0, 10:18],
    )


def solution(mesh):
    shard = P("grp", None)
    return jax.shard_map(
        per_device,
        mesh=mesh,
        in_specs=(P("rep", "grp", None), P("rep", None))
        + (shard,) * 7
        + (P("grp"),) * 4
        + (P("rep", "grp", None),),
        out_specs=(P("rep", "grp", None),) * 2 + (shard,) * 7 + (P("grp"),) * 4,
        check_vma=False,
    )
```

```python
import functools
import math

import jax
import jax.numpy as jnp
from jax import lax
from jax.experimental import pallas as pl
from jax.experimental.pallas import tpu as pltpu
from jax.sharding import PartitionSpec as P

H = 16
KVH = 8
HD = 64
CH = 96
SEQ = 1536
SPANS = 16
TILE = 256
TILES = SEQ // TILE
EPS = 1e-05
THETA = 1000000.0
AXES = ("rep", "grp")
F32 = jnp.float32
BF16 = jnp.bfloat16
VMEM_LIMIT = 48 * 1024 * 1024


def coords(i):
    rep, grp = divmod(i, 8)
    return rep // 4, (rep // 2) % 2, rep % 2, grp // 4, grp % 4


def index_of(x, ylo, core, yhi, z):
    return ((x * 2 + ylo) * 2 + core) * 8 + yhi * 4 + z


def permutation(move):
    return [(i, index_of(*move(*coords(i)))) for i in range(128)]


X_UP = permutation(lambda x, a, c, b, z: ((x + 1) % 4, a, c, b, z))
X_DOWN = permutation(lambda x, a, c, b, z: ((x - 1) % 4, a, c, b, z))
Y_SWAP = permutation(lambda x, a, c, b, z: (x, 1 - a, c, b, z))
CORE_SWAP = permutation(lambda x, a, c, b, z: (x, a, 1 - c, b, z))


def send(value, perm):
    return lax.ppermute(value, AXES, perm)


def exchange_grp(value):
    return lax.all_to_all(value, "grp", 0, 0)


def to_grp(piece):
    return jnp.broadcast_to(piece[None], (8,) + piece.shape)


def x_gather(own):
    half = own.shape[0] // 2
    left = send(own, X_UP)
    right = send(own, X_DOWN)
    far_a = send(left[:half], X_UP)
    far_b = send(right[half:], X_DOWN)
    return own, left, right, jnp.concatenate([far_a, far_b], axis=0)


def x_reduce(parts):
    own, left, right, far = parts
    half = own.shape[0] // 2
    far = far.astype(BF16)
    got_a = send(far[:half], X_UP)
    got_b = send(far[half:], X_DOWN)
    right = jnp.concatenate([right[:half] + got_a.astype(F32), right[half:]], axis=0)
    left = jnp.concatenate([left[:half], left[half:] + got_b.astype(F32)], axis=0)
    from_left = send(right.astype(BF16), X_UP)
    from_right = send(left.astype(BF16), X_DOWN)
    return own + from_left.astype(F32) + from_right.astype(F32)


def tie(*values):
    return lax.optimization_barrier(values)


def rms_norm(values, gain):
    return values * lax.rsqrt(jnp.mean(values * values, axis=-1, keepdims=True) + EPS) * gain


def rotary():
    ladder = jnp.arange(HD // 2, dtype=F32) * (2.0 / HD)
    freq = jnp.exp(-math.log(THETA) * ladder)
    angle = jnp.arange(SEQ, dtype=F32)[None, :] * freq[:, None]
    return jnp.cos(angle), jnp.sin(angle)


def mask_tile():
    key = lax.broadcasted_iota(jnp.int32, (TILE, 2 * TILE), 0)
    query = lax.broadcasted_iota(jnp.int32, (TILE, 2 * TILE), 1)
    return key <= jnp.where(query >= TILE, query - TILE, query)


def dot(a, b):
    return jnp.dot(a, b, preferred_element_type=F32)


def span_of(i):
    return slice(i * TILE, (i + 1) * TILE)


def block_start(order_ref, c):
    return pl.multiple_of(order_ref[c] * CH, CH)


def forward_kernel(
    order_ref, tokens_ref, weight_ref, attn_gain_ref, head_gain_ref, cos_ref, sin_ref,
    mixed_ref, input_ref, cols_ref, rows_ref, lin_t_ref, out_t_ref, log_ref,
    lin_rows, keys, mixed_rows,
):
    for j in range(4):
        part = slice(j * 4 * CH, (j + 1) * 4 * CH)
        x = tokens_ref[part, :].astype(F32)
        r = lax.rsqrt(jnp.mean(x * x, axis=1, keepdims=True) + EPS)
        normed = (x * r * attn_gain_ref[...]).astype(BF16)
        input_ref[part, :] = normed
        lin = dot(normed, weight_ref[...])
        for k in range(4):
            lin_rows[pl.ds(block_start(order_ref, 4 * j + k), CH), :] = lin[k * CH : (k + 1) * CH, :]
    for i in range(TILES):
        span = span_of(i)
        lin_t = lin_rows[span, :].T
        lin_t_ref[:, span] = lin_t[0:192, :]
        cosine, sine = cos_ref[:, span], sin_ref[:, span]
        parts = []
        for h, kind, scale in ((0, 0, HD ** (-0.5)), (1, 0, HD ** (-0.5)), (2, 1, 1.0)):
            u = lin_t[h * 64 : (h + 1) * 64, :]
            r = lax.rsqrt(jnp.mean(u * u, axis=0, keepdims=True) + EPS)
            n = u * r * head_gain_ref[:, kind : kind + 1]
            low, high = n[:32, :], n[32:, :]
            parts += [(low * cosine - high * sine) * scale, (high * cosine + low * sine) * scale]
        both = jnp.concatenate(parts + [lin_t[192:256, :]], axis=0)
        cols_ref[:, span] = both.astype(BF16)
        flat = both.T.astype(BF16)
        rows_ref[span, :] = flat
        keys[span, :] = flat[:, 128:192]
    mask = mask_tile()
    for i in range(TILES):
        span = span_of(i)
        query = jnp.concatenate([cols_ref[0:64, span], cols_ref[64:128, span]], axis=1)
        total = jnp.zeros((64, 2 * TILE), F32)
        weight = jnp.zeros((1, 2 * TILE), F32)
        for c in range(i + 1):
            key_span = span_of(c)
            expo = jnp.exp(dot(keys[key_span, :], query))
            if c == i:
                expo = jnp.where(mask, expo, 0.0)
            weight = weight + jnp.sum(expo, axis=0, keepdims=True)
            total = total + dot(cols_ref[192:256, key_span], expo.astype(BF16))
        total = total / weight
        logs = jnp.log(weight)
        out_t_ref[0:64, span] = total[:, :TILE]
        out_t_ref[64:128, span] = total[:, TILE:]
        log_ref[0:1, span] = logs[:, :TILE]
        log_ref[1:2, span] = logs[:, TILE:]
        mixed_rows[span, :] = (
            jnp.concatenate([total[:, :TILE], total[:, TILE:]], axis=0).T.astype(BF16)
        )
    log_ref[2:8, :] = jnp.zeros((6, SEQ), F32)
    for c in range(SPANS):
        mixed_ref[c * CH : (c + 1) * CH, :] = mixed_rows[pl.ds(block_start(order_ref, c), CH), :]


VMEM_SPEC = pl.BlockSpec(memory_space=pltpu.VMEM)
SMEM_SPEC = pl.BlockSpec(memory_space=pltpu.SMEM)


def attend_forward(order, tokens, weight, attn_gain, head_gain, cosine, sine):
    return pl.pallas_call(
        forward_kernel,
        out_shape=(
            jax.ShapeDtypeStruct((SEQ, 128), BF16),
            jax.ShapeDtypeStruct((SEQ, 1024), BF16),
            jax.ShapeDtypeStruct((256, SEQ), BF16),
            jax.ShapeDtypeStruct((SEQ, 256), BF16),
            jax.ShapeDtypeStruct((192, SEQ), F32),
            jax.ShapeDtypeStruct((128, SEQ), F32),
            jax.ShapeDtypeStruct((8, SEQ), F32),
        ),
        in_specs=[SMEM_SPEC] + [VMEM_SPEC] * 6,
        out_specs=(VMEM_SPEC,) * 7,
        scratch_shapes=[
            pltpu.VMEM((SEQ, 256), F32),
            pltpu.VMEM((SEQ, 64), BF16),
            pltpu.VMEM((SEQ, 128), BF16),
        ],
        compiler_params=pltpu.CompilerParams(vmem_limit_bytes=VMEM_LIMIT),
        cost_estimate=pl.CostEstimate(
            flops=6 * 10**9, bytes_accessed=14 * 10**6, transcendentals=3 * 10**6
        ),
        name="attend_forward",
    )(order, tokens, weight, attn_gain, head_gain, cosine, sine)


def backward_kernel(
    order_ref, cols_ref, rows_ref, grad_ref, out_t_ref, log_ref, lin_t_ref, head_gain_ref,
    cos_ref, sin_ref, result_ref, gain_ref,
    grad_rows, grad_cols, keys, values, grad_keys, grad_values, grad_query, result_rows,
):
    for c in range(SPANS):
        grad_rows[pl.ds(block_start(order_ref, c), CH), :] = grad_ref[c * CH : (c + 1) * CH, :]
    for i in range(TILES):
        span = span_of(i)
        grad_cols[:, span] = grad_rows[span, :].astype(F32).T.astype(BF16)
        keys[span, :] = rows_ref[span, 128:192]
        values[span, :] = rows_ref[span, 192:256]
    grad_keys[...] = jnp.zeros_like(grad_keys)
    grad_values[...] = jnp.zeros_like(grad_values)
    mask = mask_tile()
    scale = HD ** (-0.5)
    for i in range(TILES):
        span = span_of(i)
        query = jnp.concatenate([cols_ref[0:64, span], cols_ref[64:128, span]], axis=1)
        grad = jnp.concatenate([grad_cols[0:64, span], grad_cols[64:128, span]], axis=1)
        query_rows = jnp.concatenate([rows_ref[span, 0:64], rows_ref[span, 64:128]], axis=0)
        grad_tile = jnp.concatenate([grad_rows[span, 0:64], grad_rows[span, 64:128]], axis=0)
        logs = jnp.concatenate([log_ref[0:1, span], log_ref[1:2, span]], axis=1)
        out_t = jnp.concatenate([out_t_ref[0:64, span], out_t_ref[64:128, span]], axis=1)
        inner = jnp.sum(out_t * grad.astype(F32), axis=0, keepdims=True)
        total = jnp.zeros((64, 2 * TILE), F32)
        for c in range(i + 1):
            key_span = span_of(c)
            attend = jnp.exp(dot(keys[key_span, :], query) - logs)
            if c == i:
                attend = jnp.where(mask, attend, 0.0)
            grad_values[key_span, :] += dot(attend.astype(BF16), grad_tile)
            grad_attend = dot(values[key_span, :], grad)
            grad_scores = (attend * (grad_attend - inner)).astype(BF16)
            grad_keys[key_span, :] += dot(grad_scores, query_rows)
            total = total + dot(cols_ref[128:192, key_span], grad_scores)
        total = total * scale
        grad_query[0:64, span] = total[:, :TILE]
        grad_query[64:128, span] = total[:, TILE:]
    sums = [jnp.zeros((64, TILE), F32), jnp.zeros((64, TILE), F32)]
    for i in range(TILES):
        span = span_of(i)
        cosine, sine = cos_ref[:, span], sin_ref[:, span]
        grads = (grad_query[0:64, span], grad_query[64:128, span], grad_keys[span, :].T)
        parts = []
        for h, kind in ((0, 0), (1, 0), (2, 1)):
            low, high = grads[h][:32, :], grads[h][32:, :]
            g = jnp.concatenate([low * cosine + high * sine, high * cosine - low * sine], axis=0)
            u = lin_t_ref[h * 64 : (h + 1) * 64, span]
            r = lax.rsqrt(jnp.mean(u * u, axis=0, keepdims=True) + EPS)
            wg = g * head_gain_ref[:, kind : kind + 1]
            mean = jnp.mean(u * wg, axis=0, keepdims=True)
            parts.append(wg * r - u * (r * r * r * mean))
            sums[kind] = sums[kind] + g * u * r
        flat = jnp.concatenate(parts, axis=0).T
        result_rows[span, :] = jnp.concatenate([flat, grad_values[span, :]], axis=1).astype(BF16)
    for kind in range(2):
        gain_ref[:, kind * 128 : (kind + 1) * 128] = jnp.broadcast_to(
            jnp.sum(sums[kind], axis=1, keepdims=True), (64, 128)
        )
    for c in range(SPANS):
        result_ref[c * CH : (c + 1) * CH, :] = result_rows[pl.ds(block_start(order_ref, c), CH), :]


def attend_backward(order, cols, rows, grad, out_t, logs, lin_t, head_gain, cosine, sine):
    return pl.pallas_call(
        backward_kernel,
        out_shape=(
            jax.ShapeDtypeStruct((SEQ, 256), BF16),
            jax.ShapeDtypeStruct((64, 256), F32),
        ),
        in_specs=[SMEM_SPEC] + [VMEM_SPEC] * 9,
        out_specs=(VMEM_SPEC,) * 2,
        scratch_shapes=[
            pltpu.VMEM((SEQ, 128), BF16),
            pltpu.VMEM((128, SEQ), BF16),
            pltpu.VMEM((SEQ, 64), BF16),
            pltpu.VMEM((SEQ, 64), BF16),
            pltpu.VMEM((SEQ, 64), F32),
            pltpu.VMEM((SEQ, 64), F32),
            pltpu.VMEM((128, SEQ), F32),
            pltpu.VMEM((SEQ, 256), BF16),
        ],
        compiler_params=pltpu.CompilerParams(vmem_limit_bytes=VMEM_LIMIT),
        cost_estimate=pl.CostEstimate(
            flops=10 * 10**9, bytes_accessed=8 * 10**6, transcendentals=3 * 10**6
        ),
        name="attend_backward",
    )(order, cols, rows, grad, out_t, logs, lin_t, head_gain, cosine, sine)


def spread_kernel(index_ref, mine_ref, other_ref, down_mine_ref, down_other_ref, gate_ref, up_ref, down_ref):
    core = index_ref[4]
    for x in range(4):
        for source, down_source, place in (
            (mine_ref, down_mine_ref, core),
            (other_ref, down_other_ref, 1 - core),
        ):
            block = source[index_ref[x]].astype(F32)
            rows = pl.ds(pl.multiple_of(place * 64, 64), 64)
            for k, target in enumerate((gate_ref, up_ref)):
                for g in range(8):
                    start = g * 576 + x * 144
                    target[rows, start : start + 144] = block[
                        :, k * 1152 + g * 144 : k * 1152 + (g + 1) * 144
                    ]
            down_rows = pl.ds(pl.multiple_of(x * 144 + place * 72, 8), 72)
            down_ref[down_rows, :] = down_source[index_ref[x]].astype(F32)


def spread_slices(index, mine, other, down_mine, down_other):
    return pl.pallas_call(
        spread_kernel,
        out_shape=(
            jax.ShapeDtypeStruct((128, 4608), F32),
            jax.ShapeDtypeStruct((128, 4608), F32),
            jax.ShapeDtypeStruct((576, 1024), F32),
        ),
        in_specs=[SMEM_SPEC] + [VMEM_SPEC] * 4,
        out_specs=(VMEM_SPEC,) * 3,
        compiler_params=pltpu.CompilerParams(vmem_limit_bytes=VMEM_LIMIT),
        cost_estimate=pl.CostEstimate(flops=10**7, bytes_accessed=10**7, transcendentals=0),
        name="spread_slices",
    )(index, mine, other, down_mine, down_other)


def swiglu(gate_in, up_in):
    return jax.nn.silu(gate_in) * up_in


def per_device(
    tokens, span_order, query_weight, key_weight, value_weight, out_weight,
    gate_weight, up_weight, down_weight, attn_gain, ffn_gain, query_gain, key_gain, cotangent,
):
    rep = lax.axis_index("rep")
    place = lax.axis_index("grp")
    xpos, core = rep // 4, rep % 2
    rows = tokens.shape[1]
    order_row = span_order[0]

    def core_half(matrix):
        half = matrix.shape[0] // 2
        return lax.dynamic_slice_in_dim(matrix, core * half, half, 0)

    def both_cores(mine):
        other = send(mine, CORE_SWAP)
        picked = lax.broadcasted_iota(jnp.int32, (1, 2, 1, 1), 1) == core
        return jnp.where(picked, mine[:, None], other[:, None]).reshape(-1, mine.shape[-1])

    grouped = jnp.concatenate(
        [
            query_weight.reshape(128, KVH, 128),
            key_weight.reshape(128, KVH, HD),
            value_weight.reshape(128, KVH, HD),
        ],
        axis=2,
    )
    gain_rows = jnp.concatenate(
        [
            jnp.concatenate([attn_gain, ffn_gain])[None],
            jnp.concatenate([query_gain, key_gain, jnp.zeros((240,), BF16)])[None],
            jnp.zeros((14, 256), BF16),
        ],
        axis=0,
    )
    got = exchange_grp(
        jnp.concatenate(
            [grouped.transpose(1, 0, 2), jnp.broadcast_to(gain_rows[None], (8, 16, 256))], axis=1
        )
    )
    all_tokens = lax.all_gather(tokens[0], "grp", axis=0, tiled=True)
    def x_columns(matrix):
        cut = matrix.reshape(128, 8, 4, 144)
        return lax.dynamic_index_in_dim(cut, xpos, 2, keepdims=False).reshape(128, 1152)

    gate_up_piece = core_half(jnp.concatenate([x_columns(gate_weight), x_columns(up_weight)], axis=1))
    down_piece = core_half(
        lax.dynamic_index_in_dim(down_weight.reshape(4, 144, 1024), xpos, 0, keepdims=False)
    )
    out_sent, got = tie(to_grp(core_half(out_weight)), got)
    out_half_weight = exchange_grp(out_sent)
    gate_up_sent, down_sent, qkv_sent, out_half_weight = tie(
        to_grp(gate_up_piece),
        to_grp(down_piece),
        to_grp(core_half(grouped.reshape(128, 2048))),
        out_half_weight,
    )
    down_half = exchange_grp(down_sent)

    cot = jnp.concatenate(x_gather(cotangent[0]), axis=0)

    head_weight = got[:, :128].reshape(1024, 256)
    attn_scale = got[:, 128, :128].reshape(1024).astype(F32)
    ffn_scale = got[:, 128, 128:].reshape(1024).astype(F32)
    head_gain = jnp.stack(
        [got[:, 129, 0:8].reshape(HD), got[:, 129, 8:16].reshape(HD)], axis=1
    ).astype(F32)
    x_in = tokens[0].astype(F32)
    cosine, sine = rotary()
    mixed_heads, input_attn, cols, rows_sorted, lin_t, out_t, logs = attend_forward(
        order_row, all_tokens, head_weight, attn_scale[None], head_gain, cosine, sine
    )
    mixed_heads, out_full, cot, down_half = tie(
        mixed_heads, both_cores(out_half_weight), cot, down_half
    )
    mixed = exchange_grp(mixed_heads.reshape(8, rows, 128))
    mixed, gate_up_sent = tie(mixed, gate_up_sent)
    gate_up_half = exchange_grp(gate_up_sent)
    mixed = mixed.transpose(1, 0, 2).reshape(rows, 1024)
    x_mid = x_in + dot(mixed, out_full)

    input_ffn_own = rms_norm(x_mid, ffn_scale).astype(BF16)
    input_ffn = jnp.concatenate(x_gather(input_ffn_own), axis=0)
    down_full = both_cores(down_half)
    qkv_sent, gate_up_half, input_ffn = tie(qkv_sent, gate_up_half, input_ffn)
    qkv_half = exchange_grp(qkv_sent)
    gate_up_full = both_cores(gate_up_half)

    def core_sum(full, half):
        low = full.astype(BF16).reshape(8, 2, half, full.shape[-1])
        mine = lax.dynamic_index_in_dim(low, core, 1, keepdims=False)
        theirs = lax.dynamic_index_in_dim(low, 1 - core, 1, keepdims=False)
        return (mine.astype(F32) + send(theirs, CORE_SWAP).astype(F32)).astype(BF16)

    def y_sum(value):
        return (value.astype(F32) + send(value, Y_SWAP).astype(F32)).astype(BF16)

    def total(value):
        return jnp.sum(value.astype(F32), axis=0).astype(BF16)

    gate_up = dot(input_ffn, gate_up_full)
    gate, up_value = gate_up[:, :1152], gate_up[:, 1152:]
    hidden_exact, pull_swiglu = jax.vjp(swiglu, gate, up_value)
    hidden = hidden_exact.astype(BF16)
    down_grad = jnp.einsum("tf,td->fd", hidden, cot, preferred_element_type=F32)
    down_sent = core_sum(down_grad, 72)
    grad_hidden = jnp.einsum("td,fd->tf", cot, down_full, preferred_element_type=F32)
    grad_gate, grad_up = pull_swiglu(grad_hidden)
    grad_gate_up = jnp.concatenate([grad_gate.astype(BF16), grad_up.astype(BF16)], axis=1)
    grad_gate_up, down_sent, qkv_half = tie(grad_gate_up, down_sent, qkv_half)
    down_got = exchange_grp(down_sent)
    gate_up_grad = jnp.einsum("td,tf->df", input_ffn, grad_gate_up, preferred_element_type=F32)
    gate_up_sent = core_sum(gate_up_grad, 64)
    grad_input_part = jnp.einsum(
        "tf,df->td", grad_gate_up, gate_up_full, preferred_element_type=F32
    )
    grad_input_part, gate_up_sent, down_got = tie(grad_input_part, gate_up_sent, down_got)
    gate_up_got = exchange_grp(gate_up_sent)
    grad_input_ffn = x_reduce(grad_input_part.reshape(4, rows, 1024))
    grad_input_ffn, gate_up_got = tie(grad_input_ffn, gate_up_got)
    down_part = dot(hidden, down_full)

    _, pull_ffn_norm = jax.vjp(rms_norm, x_mid, ffn_scale)
    grad_mid_norm, ffn_gain_grad = pull_ffn_norm(grad_input_ffn)
    grad_mid = cotangent[0].astype(F32) + grad_mid_norm
    grad_attn = grad_mid.astype(BF16)
    grad_mixed = jnp.einsum(
        "td,fd->tf", grad_attn, out_full, preferred_element_type=F32
    ).astype(BF16)
    grad_sent, grad_attn, gate_up_got, down_got = tie(
        grad_mixed.reshape(rows, 8, 128).transpose(1, 0, 2), grad_attn, gate_up_got, down_got
    )
    grad_heads = exchange_grp(grad_sent)
    out_grad = jnp.einsum("tf,td->fd", mixed, grad_attn, preferred_element_type=F32)
    gate_up_sum = y_sum(total(gate_up_got))
    down_sum = y_sum(total(down_got))
    out_sent = core_sum(out_grad, 64)
    grad_heads, out_sent, gate_up_sum, down_sum = tie(
        grad_heads, out_sent, gate_up_sum, down_sum
    )
    out_got = exchange_grp(out_sent)
    gate_up_parts = x_gather(gate_up_sum)
    down_parts = x_gather(down_sum)
    grad_lin, head_gain_grad = attend_backward(
        order_row, cols, rows_sorted, grad_heads.reshape(SEQ, 128), out_t, logs, lin_t,
        head_gain, cosine, sine,
    )
    qkv_grad = jnp.einsum("td,tf->df", input_attn, grad_lin, preferred_element_type=F32)
    grad_lin, out_got, down_part = tie(grad_lin, out_got, down_part)
    outputs = (x_mid + x_reduce(down_part.reshape(4, rows, 1024))).astype(BF16)[None]
    attn_gain_part = jnp.sum(qkv_grad * head_weight.astype(F32), axis=1) / attn_scale
    gain_parts = jnp.concatenate(
        [
            jnp.concatenate(
                [attn_gain_part.reshape(8, 1, 128), ffn_gain_grad.reshape(8, 1, 128)], axis=2
            ),
            jnp.concatenate(
                [
                    head_gain_grad[:, 0].reshape(8, 1, 8),
                    head_gain_grad[:, 128].reshape(8, 1, 8),
                    jnp.zeros((8, 1, 240), F32),
                ],
                axis=2,
            ),
            jnp.zeros((8, 14, 256), F32),
        ],
        axis=1,
    )
    packed = exchange_grp(grad_lin.reshape(8, rows, 256))
    qkv_sent = jnp.concatenate(
        [qkv_grad.astype(BF16).reshape(8, 128, 256), gain_parts.astype(BF16)], axis=1
    )
    qkv_sent, packed = tie(qkv_sent, packed)
    qkv_got = exchange_grp(qkv_sent)
    qkv_got, gate_up_parts, down_parts = tie(qkv_got, gate_up_parts, down_parts)
    grad_packed = packed.transpose(1, 0, 2)
    qkv_rows = qkv_got[:, :128]
    out_sum = jnp.sum(out_got.astype(F32), axis=0).astype(BF16)
    qkv_full = both_cores(qkv_half)
    grad_input_attn = jnp.einsum(
        "tf,df->td", grad_packed.reshape(rows, 2048), qkv_full, preferred_element_type=F32
    )
    _, pull_attn_norm = jax.vjp(lambda v: rms_norm(v, attn_scale), x_in)
    (grad_in_norm,) = pull_attn_norm(grad_input_attn)
    input_grad = (grad_mid + grad_in_norm)[None]

    gain_got = jnp.sum(qkv_got[:, 128:].astype(F32), axis=0)
    gain_owned = jnp.stack(
        [
            gain_got[0, :128],
            gain_got[0, 128:],
            jnp.pad(gain_got[1, 0:8], (0, 120)),
            jnp.pad(gain_got[1, 8:16], (0, 120)),
        ]
    )
    gain_columns = jnp.pad(gain_owned.T, ((0, 0), (0, 252))).astype(BF16)

    own_half = lax.dynamic_update_slice(jnp.zeros((128, 1024), BF16), out_sum, (core * 64, 0))
    attn_rows = jnp.concatenate(
        [qkv_rows.reshape(8, 16, 8, 256).transpose(1, 0, 2, 3).reshape(16, 64, 256)]
        + [own_half[:, k * 256 : (k + 1) * 256].reshape(16, 8, 256) for k in range(4)]
        + [gain_columns.reshape(16, 8, 256)],
        axis=1,
    )
    attn_part = jnp.sum(lax.all_to_all(attn_rows, "rep", 0, 0).astype(F32), axis=0).astype(BF16)
    attn_all = lax.all_to_all(
        jnp.broadcast_to(attn_part[None], (16, 104, 256)), "rep", 0, 0
    )
    heads_all = attn_all[:, :64].reshape(16, 8, 8, 256)

    def by_head(start, stop):
        width = stop - start
        cut = heads_all[:, :, :, start:stop].transpose(0, 2, 1, 3)
        return cut.reshape(128, 8 * width).astype(F32)

    out_all = jnp.concatenate(
        [attn_all[:, 64 + 8 * k : 72 + 8 * k].reshape(128, 256) for k in range(4)], axis=1
    ).astype(F32)
    gain_all = attn_all[:, 96:104].reshape(128, 256).astype(F32)

    gate_up_mine = jnp.stack(gate_up_parts)
    down_mine = jnp.stack(down_parts)
    gate_all, up_all, down_all = spread_slices(
        jnp.concatenate(
            [jnp.array([0, 2, 3, 1], jnp.int32)[(jnp.arange(4) - xpos) % 4], core[None]]
        ),
        gate_up_mine,
        send(gate_up_mine, CORE_SWAP),
        down_mine,
        send(down_mine, CORE_SWAP),
    )
    return (
        outputs,
        input_grad,
        by_head(0, 128),
        by_head(128, 192),
        by_head(192, 256),
        out_all,
        gate_all,
        up_all,
        down_all,
        gain_all[:, 0],
        gain_all[:, 1],
        gain_all[:8, 2],
        gain_all[:8, 3],
    )


def solution(mesh):
    shard = P("grp", None)
    return jax.shard_map(
        per_device,
        mesh=mesh,
        in_specs=(P("rep", "grp", None), P("rep", None))
        + (shard,) * 7
        + (P("grp"),) * 4
        + (P("rep", "grp", None),),
        out_specs=(P("rep", "grp", None),) * 2 + (shard,) * 7 + (P("grp"),) * 4,
        check_vma=False,
    )
```

```python
import functools
import math

import jax
import jax.numpy as jnp
from jax import lax
from jax.experimental import pallas as pl
from jax.experimental.pallas import tpu as pltpu
from jax.sharding import PartitionSpec as P

H = 16
KVH = 8
HD = 64
CH = 96
SEQ = 1536
SPANS = 16
TILE = 256
TILES = SEQ // TILE
EPS = 1e-05
THETA = 1000000.0
AXES = ("rep", "grp")
F32 = jnp.float32
BF16 = jnp.bfloat16
VMEM_LIMIT = 48 * 1024 * 1024


def coords(i):
    rep, grp = divmod(i, 8)
    return rep // 4, (rep // 2) % 2, rep % 2, grp // 4, grp % 4


def index_of(x, ylo, core, yhi, z):
    return ((x * 2 + ylo) * 2 + core) * 8 + yhi * 4 + z


def permutation(move):
    return [(i, index_of(*move(*coords(i)))) for i in range(128)]


X_UP = permutation(lambda x, a, c, b, z: ((x + 1) % 4, a, c, b, z))
X_DOWN = permutation(lambda x, a, c, b, z: ((x - 1) % 4, a, c, b, z))
Y_SWAP = permutation(lambda x, a, c, b, z: (x, 1 - a, c, b, z))
CORE_SWAP = permutation(lambda x, a, c, b, z: (x, a, 1 - c, b, z))


def send(value, perm):
    return lax.ppermute(value, AXES, perm)


def exchange_grp(value):
    return lax.all_to_all(value, "grp", 0, 0)


def to_grp(piece):
    return jnp.broadcast_to(piece[None], (8,) + piece.shape)


def x_gather(own):
    half = own.shape[0] // 2
    left = send(own, X_UP)
    right = send(own, X_DOWN)
    far_a = send(left[:half], X_UP)
    far_b = send(right[half:], X_DOWN)
    return own, left, right, jnp.concatenate([far_a, far_b], axis=0)


def x_reduce(parts):
    own, left, right, far = parts
    half = own.shape[0] // 2
    far = far.astype(BF16)
    got_a = send(far[:half], X_UP)
    got_b = send(far[half:], X_DOWN)
    right = jnp.concatenate([right[:half] + got_a.astype(F32), right[half:]], axis=0)
    left = jnp.concatenate([left[:half], left[half:] + got_b.astype(F32)], axis=0)
    from_left = send(right.astype(BF16), X_UP)
    from_right = send(left.astype(BF16), X_DOWN)
    return own + from_left.astype(F32) + from_right.astype(F32)


def tie(*values):
    return lax.optimization_barrier(values)


def rms_norm(values, gain):
    return values * lax.rsqrt(jnp.mean(values * values, axis=-1, keepdims=True) + EPS) * gain


def rotary():
    ladder = jnp.arange(HD // 2, dtype=F32) * (2.0 / HD)
    freq = jnp.exp(-math.log(THETA) * ladder)
    angle = jnp.arange(SEQ, dtype=F32)[None, :] * freq[:, None]
    return jnp.cos(angle), jnp.sin(angle)


def mask_tile():
    key = lax.broadcasted_iota(jnp.int32, (TILE, 2 * TILE), 0)
    query = lax.broadcasted_iota(jnp.int32, (TILE, 2 * TILE), 1)
    return key <= jnp.where(query >= TILE, query - TILE, query)


def dot(a, b):
    return jnp.dot(a, b, preferred_element_type=F32)


def span_of(i):
    return slice(i * TILE, (i + 1) * TILE)


def block_start(order_ref, c):
    return pl.multiple_of(order_ref[c] * CH, CH)


def forward_kernel(
    order_ref, tokens_ref, weight_ref, attn_gain_ref, head_gain_ref, cos_ref, sin_ref,
    mixed_ref, input_ref, cols_ref, rows_ref, lin_t_ref, out_t_ref, log_ref,
    lin_rows, keys, mixed_rows,
):
    for j in range(4):
        part = slice(j * 4 * CH, (j + 1) * 4 * CH)
        x = tokens_ref[part, :].astype(F32)
        r = lax.rsqrt(jnp.mean(x * x, axis=1, keepdims=True) + EPS)
        normed = (x * r * attn_gain_ref[...]).astype(BF16)
        input_ref[part, :] = normed
        lin = dot(normed, weight_ref[...])
        for k in range(4):
            lin_rows[pl.ds(block_start(order_ref, 4 * j + k), CH), :] = lin[k * CH : (k + 1) * CH, :]
    for i in range(TILES):
        span = span_of(i)
        lin_t = lin_rows[span, :].T
        lin_t_ref[:, span] = lin_t[0:192, :]
        cosine, sine = cos_ref[:, span], sin_ref[:, span]
        parts = []
        for h, kind, scale in ((0, 0, HD ** (-0.5)), (1, 0, HD ** (-0.5)), (2, 1, 1.0)):
            u = lin_t[h * 64 : (h + 1) * 64, :]
            r = lax.rsqrt(jnp.mean(u * u, axis=0, keepdims=True) + EPS)
            n = u * r * head_gain_ref[:, kind : kind + 1]
            low, high = n[:32, :], n[32:, :]
            parts += [(low * cosine - high * sine) * scale, (high * cosine + low * sine) * scale]
        both = jnp.concatenate(parts + [lin_t[192:256, :]], axis=0)
        cols_ref[:, span] = both.astype(BF16)
        flat = both.T.astype(BF16)
        rows_ref[span, :] = flat
        keys[span, :] = flat[:, 128:192]
    mask = mask_tile()
    for i in range(TILES):
        span = span_of(i)
        query = jnp.concatenate([cols_ref[0:64, span], cols_ref[64:128, span]], axis=1)
        total = jnp.zeros((64, 2 * TILE), F32)
        weight = jnp.zeros((1, 2 * TILE), F32)
        for c in range(i + 1):
            key_span = span_of(c)
            expo = jnp.exp(dot(keys[key_span, :], query))
            if c == i:
                expo = jnp.where(mask, expo, 0.0)
            weight = weight + jnp.sum(expo, axis=0, keepdims=True)
            total = total + dot(cols_ref[192:256, key_span], expo.astype(BF16))
        total = total / weight
        logs = jnp.log(weight)
        out_t_ref[0:64, span] = total[:, :TILE]
        out_t_ref[64:128, span] = total[:, TILE:]
        log_ref[0:1, span] = logs[:, :TILE]
        log_ref[1:2, span] = logs[:, TILE:]
        mixed_rows[span, :] = (
            jnp.concatenate([total[:, :TILE], total[:, TILE:]], axis=0).T.astype(BF16)
        )
    log_ref[2:8, :] = jnp.zeros((6, SEQ), F32)
    for c in range(SPANS):
        mixed_ref[c * CH : (c + 1) * CH, :] = mixed_rows[pl.ds(block_start(order_ref, c), CH), :]


VMEM_SPEC = pl.BlockSpec(memory_space=pltpu.VMEM)
SMEM_SPEC = pl.BlockSpec(memory_space=pltpu.SMEM)


def attend_forward(order, tokens, weight, attn_gain, head_gain, cosine, sine):
    return pl.pallas_call(
        forward_kernel,
        out_shape=(
            jax.ShapeDtypeStruct((SEQ, 128), BF16),
            jax.ShapeDtypeStruct((SEQ, 1024), BF16),
            jax.ShapeDtypeStruct((256, SEQ), BF16),
            jax.ShapeDtypeStruct((SEQ, 256), BF16),
            jax.ShapeDtypeStruct((192, SEQ), F32),
            jax.ShapeDtypeStruct((128, SEQ), F32),
            jax.ShapeDtypeStruct((8, SEQ), F32),
        ),
        in_specs=[SMEM_SPEC] + [VMEM_SPEC] * 6,
        out_specs=(VMEM_SPEC,) * 7,
        scratch_shapes=[
            pltpu.VMEM((SEQ, 256), F32),
            pltpu.VMEM((SEQ, 64), BF16),
            pltpu.VMEM((SEQ, 128), BF16),
        ],
        compiler_params=pltpu.CompilerParams(vmem_limit_bytes=VMEM_LIMIT),
        cost_estimate=pl.CostEstimate(
            flops=6 * 10**9, bytes_accessed=14 * 10**6, transcendentals=3 * 10**6
        ),
        name="attend_forward",
    )(order, tokens, weight, attn_gain, head_gain, cosine, sine)


def backward_kernel(
    order_ref, cols_ref, rows_ref, grad_ref, out_t_ref, log_ref, lin_t_ref, head_gain_ref,
    cos_ref, sin_ref, result_ref, gain_ref,
    grad_rows, grad_cols, keys, values, grad_keys, grad_values, grad_query, result_rows,
):
    for c in range(SPANS):
        grad_rows[pl.ds(block_start(order_ref, c), CH), :] = grad_ref[c * CH : (c + 1) * CH, :]
    for i in range(TILES):
        span = span_of(i)
        grad_cols[:, span] = grad_rows[span, :].astype(F32).T.astype(BF16)
        keys[span, :] = rows_ref[span, 128:192]
        values[span, :] = rows_ref[span, 192:256]
    grad_keys[...] = jnp.zeros_like(grad_keys)
    grad_values[...] = jnp.zeros_like(grad_values)
    mask = mask_tile()
    scale = HD ** (-0.5)
    for i in range(TILES):
        span = span_of(i)
        query = jnp.concatenate([cols_ref[0:64, span], cols_ref[64:128, span]], axis=1)
        grad = jnp.concatenate([grad_cols[0:64, span], grad_cols[64:128, span]], axis=1)
        query_rows = jnp.concatenate([rows_ref[span, 0:64], rows_ref[span, 64:128]], axis=0)
        grad_tile = jnp.concatenate([grad_rows[span, 0:64], grad_rows[span, 64:128]], axis=0)
        logs = jnp.concatenate([log_ref[0:1, span], log_ref[1:2, span]], axis=1)
        out_t = jnp.concatenate([out_t_ref[0:64, span], out_t_ref[64:128, span]], axis=1)
        inner = jnp.sum(out_t * grad.astype(F32), axis=0, keepdims=True)
        total = jnp.zeros((64, 2 * TILE), F32)
        for c in range(i + 1):
            key_span = span_of(c)
            attend = jnp.exp(dot(keys[key_span, :], query) - logs)
            if c == i:
                attend = jnp.where(mask, attend, 0.0)
            grad_values[key_span, :] += dot(attend.astype(BF16), grad_tile)
            grad_attend = dot(values[key_span, :], grad)
            grad_scores = (attend * (grad_attend - inner)).astype(BF16)
            grad_keys[key_span, :] += dot(grad_scores, query_rows)
            total = total + dot(cols_ref[128:192, key_span], grad_scores)
        total = total * scale
        grad_query[0:64, span] = total[:, :TILE]
        grad_query[64:128, span] = total[:, TILE:]
    sums = [jnp.zeros((64, TILE), F32), jnp.zeros((64, TILE), F32)]
    for i in range(TILES):
        span = span_of(i)
        cosine, sine = cos_ref[:, span], sin_ref[:, span]
        grads = (grad_query[0:64, span], grad_query[64:128, span], grad_keys[span, :].T)
        parts = []
        for h, kind in ((0, 0), (1, 0), (2, 1)):
            low, high = grads[h][:32, :], grads[h][32:, :]
            g = jnp.concatenate([low * cosine + high * sine, high * cosine - low * sine], axis=0)
            u = lin_t_ref[h * 64 : (h + 1) * 64, span]
            r = lax.rsqrt(jnp.mean(u * u, axis=0, keepdims=True) + EPS)
            wg = g * head_gain_ref[:, kind : kind + 1]
            mean = jnp.mean(u * wg, axis=0, keepdims=True)
            parts.append(wg * r - u * (r * r * r * mean))
            sums[kind] = sums[kind] + g * u * r
        flat = jnp.concatenate(parts, axis=0).T
        result_rows[span, :] = jnp.concatenate([flat, grad_values[span, :]], axis=1).astype(BF16)
    for kind in range(2):
        gain_ref[:, kind * 128 : (kind + 1) * 128] = jnp.broadcast_to(
            jnp.sum(sums[kind], axis=1, keepdims=True), (64, 128)
        )
    for c in range(SPANS):
        result_ref[c * CH : (c + 1) * CH, :] = result_rows[pl.ds(block_start(order_ref, c), CH), :]


def attend_backward(order, cols, rows, grad, out_t, logs, lin_t, head_gain, cosine, sine):
    return pl.pallas_call(
        backward_kernel,
        out_shape=(
            jax.ShapeDtypeStruct((SEQ, 256), BF16),
            jax.ShapeDtypeStruct((64, 256), F32),
        ),
        in_specs=[SMEM_SPEC] + [VMEM_SPEC] * 9,
        out_specs=(VMEM_SPEC,) * 2,
        scratch_shapes=[
            pltpu.VMEM((SEQ, 128), BF16),
            pltpu.VMEM((128, SEQ), BF16),
            pltpu.VMEM((SEQ, 64), BF16),
            pltpu.VMEM((SEQ, 64), BF16),
            pltpu.VMEM((SEQ, 64), F32),
            pltpu.VMEM((SEQ, 64), F32),
            pltpu.VMEM((128, SEQ), F32),
            pltpu.VMEM((SEQ, 256), BF16),
        ],
        compiler_params=pltpu.CompilerParams(vmem_limit_bytes=VMEM_LIMIT),
        cost_estimate=pl.CostEstimate(
            flops=10 * 10**9, bytes_accessed=8 * 10**6, transcendentals=3 * 10**6
        ),
        name="attend_backward",
    )(order, cols, rows, grad, out_t, logs, lin_t, head_gain, cosine, sine)


def spread_kernel(index_ref, mine_ref, other_ref, down_mine_ref, down_other_ref, gate_ref, up_ref, down_ref):
    core = index_ref[4]
    for x in range(4):
        for source, down_source, place in (
            (mine_ref, down_mine_ref, core),
            (other_ref, down_other_ref, 1 - core),
        ):
            block = source[index_ref[x]].astype(F32)
            rows = pl.ds(pl.multiple_of(place * 64, 64), 64)
            for k, target in enumerate((gate_ref, up_ref)):
                for g in range(8):
                    start = g * 576 + x * 144
                    target[rows, start : start + 144] = block[
                        :, k * 1152 + g * 144 : k * 1152 + (g + 1) * 144
                    ]
            down_rows = pl.ds(pl.multiple_of(x * 144 + place * 72, 8), 72)
            down_ref[down_rows, :] = down_source[index_ref[x]].astype(F32)


def spread_slices(index, mine, other, down_mine, down_other):
    return pl.pallas_call(
        spread_kernel,
        out_shape=(
            jax.ShapeDtypeStruct((128, 4608), F32),
            jax.ShapeDtypeStruct((128, 4608), F32),
            jax.ShapeDtypeStruct((576, 1024), F32),
        ),
        in_specs=[SMEM_SPEC] + [VMEM_SPEC] * 4,
        out_specs=(VMEM_SPEC,) * 3,
        compiler_params=pltpu.CompilerParams(vmem_limit_bytes=VMEM_LIMIT),
        cost_estimate=pl.CostEstimate(flops=10**7, bytes_accessed=10**7, transcendentals=0),
        name="spread_slices",
    )(index, mine, other, down_mine, down_other)


def swiglu(gate_in, up_in):
    return jax.nn.silu(gate_in) * up_in


def per_device(
    tokens, span_order, query_weight, key_weight, value_weight, out_weight,
    gate_weight, up_weight, down_weight, attn_gain, ffn_gain, query_gain, key_gain, cotangent,
):
    rep = lax.axis_index("rep")
    place = lax.axis_index("grp")
    xpos, core = rep // 4, rep % 2
    rows = tokens.shape[1]
    order_row = span_order[0]

    def core_half(matrix):
        half = matrix.shape[0] // 2
        return lax.dynamic_slice_in_dim(matrix, core * half, half, 0)

    def both_cores(mine):
        other = send(mine, CORE_SWAP)
        picked = lax.broadcasted_iota(jnp.int32, (1, 2, 1, 1), 1) == core
        return jnp.where(picked, mine[:, None], other[:, None]).reshape(-1, mine.shape[-1])

    grouped = jnp.concatenate(
        [
            query_weight.reshape(128, KVH, 128),
            key_weight.reshape(128, KVH, HD),
            value_weight.reshape(128, KVH, HD),
        ],
        axis=2,
    )
    gain_rows = jnp.concatenate(
        [
            jnp.concatenate([attn_gain, ffn_gain])[None],
            jnp.concatenate([query_gain, key_gain, jnp.zeros((240,), BF16)])[None],
            jnp.zeros((14, 256), BF16),
        ],
        axis=0,
    )
    got = exchange_grp(
        jnp.concatenate(
            [grouped.transpose(1, 0, 2), jnp.broadcast_to(gain_rows[None], (8, 16, 256))], axis=1
        )
    )
    all_tokens = lax.all_gather(tokens[0], "grp", axis=0, tiled=True)
    def x_columns(matrix):
        cut = matrix.reshape(128, 8, 4, 144)
        return lax.dynamic_index_in_dim(cut, xpos, 2, keepdims=False).reshape(128, 1152)

    gate_up_piece = core_half(jnp.concatenate([x_columns(gate_weight), x_columns(up_weight)], axis=1))
    down_piece = core_half(
        lax.dynamic_index_in_dim(down_weight.reshape(4, 144, 1024), xpos, 0, keepdims=False)
    )
    out_sent, got = tie(to_grp(core_half(out_weight)), got)
    out_half_weight = exchange_grp(out_sent)
    gate_up_sent, down_sent, qkv_sent, out_half_weight = tie(
        to_grp(gate_up_piece),
        to_grp(down_piece),
        to_grp(core_half(grouped.reshape(128, 2048))),
        out_half_weight,
    )
    down_half = exchange_grp(down_sent)

    cot = jnp.concatenate(x_gather(cotangent[0]), axis=0)

    head_weight = got[:, :128].reshape(1024, 256)
    attn_scale = got[:, 128, :128].reshape(1024).astype(F32)
    ffn_scale = got[:, 128, 128:].reshape(1024).astype(F32)
    head_gain = jnp.stack(
        [got[:, 129, 0:8].reshape(HD), got[:, 129, 8:16].reshape(HD)], axis=1
    ).astype(F32)
    x_in = tokens[0].astype(F32)
    cosine, sine = rotary()
    mixed_heads, input_attn, cols, rows_sorted, lin_t, out_t, logs = attend_forward(
        order_row, all_tokens, head_weight, attn_scale[None], head_gain, cosine, sine
    )
    mixed_heads, out_full, cot, down_half = tie(
        mixed_heads, both_cores(out_half_weight), cot, down_half
    )
    mixed = exchange_grp(mixed_heads.reshape(8, rows, 128))
    mixed, gate_up_sent = tie(mixed, gate_up_sent)
    gate_up_half = exchange_grp(gate_up_sent)
    mixed = mixed.transpose(1, 0, 2).reshape(rows, 1024)
    x_mid = x_in + dot(mixed, out_full)

    input_ffn_own = rms_norm(x_mid, ffn_scale).astype(BF16)
    input_ffn = jnp.concatenate(x_gather(input_ffn_own), axis=0)
    qkv_sent, gate_up_half, input_ffn, down_full = tie(
        qkv_sent, gate_up_half, input_ffn, both_cores(down_half)
    )
    qkv_half = exchange_grp(qkv_sent)
    gate_up_full = both_cores(gate_up_half)

    def core_sum(full, half):
        low = full.astype(BF16).reshape(8, 2, half, full.shape[-1])
        mine = lax.dynamic_index_in_dim(low, core, 1, keepdims=False)
        theirs = lax.dynamic_index_in_dim(low, 1 - core, 1, keepdims=False)
        return (mine.astype(F32) + send(theirs, CORE_SWAP).astype(F32)).astype(BF16)

    def y_sum(value):
        return (value.astype(F32) + send(value, Y_SWAP).astype(F32)).astype(BF16)

    def total(value):
        return jnp.sum(value.astype(F32), axis=0).astype(BF16)

    gate_up = dot(input_ffn, gate_up_full)
    gate, up_value = gate_up[:, :1152], gate_up[:, 1152:]
    hidden_exact, pull_swiglu = jax.vjp(swiglu, gate, up_value)
    hidden = hidden_exact.astype(BF16)
    down_grad = jnp.einsum("tf,td->fd", hidden, cot, preferred_element_type=F32)
    down_sent = core_sum(down_grad, 72)
    grad_hidden = jnp.einsum("td,fd->tf", cot, down_full, preferred_element_type=F32)
    grad_gate, grad_up = pull_swiglu(grad_hidden)
    grad_gate_up = jnp.concatenate([grad_gate.astype(BF16), grad_up.astype(BF16)], axis=1)
    grad_gate_up, down_sent, qkv_half = tie(grad_gate_up, down_sent, qkv_half)
    down_got = exchange_grp(down_sent)
    gate_up_grad = jnp.einsum("td,tf->df", input_ffn, grad_gate_up, preferred_element_type=F32)
    gate_up_sent = core_sum(gate_up_grad, 64)
    grad_input_part = jnp.einsum(
        "tf,df->td", grad_gate_up, gate_up_full, preferred_element_type=F32
    )
    grad_input_part, gate_up_sent, down_got = tie(grad_input_part, gate_up_sent, down_got)
    gate_up_got = exchange_grp(gate_up_sent)
    grad_input_ffn = x_reduce(grad_input_part.reshape(4, rows, 1024))
    grad_input_ffn, gate_up_got, down_sum, down_part = tie(
        grad_input_ffn, gate_up_got, total(down_got), dot(hidden, down_full)
    )

    _, pull_ffn_norm = jax.vjp(rms_norm, x_mid, ffn_scale)
    grad_mid_norm, ffn_gain_grad = pull_ffn_norm(grad_input_ffn)
    grad_mid = cotangent[0].astype(F32) + grad_mid_norm
    grad_attn = grad_mid.astype(BF16)
    grad_mixed = jnp.einsum(
        "td,fd->tf", grad_attn, out_full, preferred_element_type=F32
    ).astype(BF16)
    grad_sent, grad_attn, gate_up_got = tie(
        grad_mixed.reshape(rows, 8, 128).transpose(1, 0, 2), grad_attn, gate_up_got
    )
    grad_heads = exchange_grp(grad_sent)
    out_grad = jnp.einsum("tf,td->fd", mixed, grad_attn, preferred_element_type=F32)
    gate_up_sum = y_sum(total(gate_up_got))
    down_sum = y_sum(down_sum)
    out_sent = core_sum(out_grad, 64)
    grad_heads, out_sent, gate_up_sum, down_sum = tie(
        grad_heads, out_sent, gate_up_sum, down_sum
    )
    out_got = exchange_grp(out_sent)
    gate_up_parts = x_gather(gate_up_sum)
    down_parts = x_gather(down_sum)
    grad_lin, head_gain_grad = attend_backward(
        order_row, cols, rows_sorted, grad_heads.reshape(SEQ, 128), out_t, logs, lin_t,
        head_gain, cosine, sine,
    )
    qkv_grad = jnp.einsum("td,tf->df", input_attn, grad_lin, preferred_element_type=F32)
    grad_lin, out_got, down_part = tie(grad_lin, out_got, down_part)
    outputs = (x_mid + x_reduce(down_part.reshape(4, rows, 1024))).astype(BF16)[None]
    attn_gain_part = jnp.sum(qkv_grad * head_weight.astype(F32), axis=1) / attn_scale
    gain_parts = jnp.concatenate(
        [
            jnp.concatenate(
                [attn_gain_part.reshape(8, 1, 128), ffn_gain_grad.reshape(8, 1, 128)], axis=2
            ),
            jnp.concatenate(
                [
                    head_gain_grad[:, 0].reshape(8, 1, 8),
                    head_gain_grad[:, 128].reshape(8, 1, 8),
                    jnp.zeros((8, 1, 240), F32),
                ],
                axis=2,
            ),
            jnp.zeros((8, 14, 256), F32),
        ],
        axis=1,
    )
    packed = exchange_grp(grad_lin.reshape(8, rows, 256))
    qkv_sent = jnp.concatenate(
        [qkv_grad.astype(BF16).reshape(8, 128, 256), gain_parts.astype(BF16)], axis=1
    )
    qkv_sent, packed, qkv_half = tie(qkv_sent, packed, qkv_half)
    qkv_got = exchange_grp(qkv_sent)
    qkv_got, gate_up_parts, down_parts = tie(qkv_got, gate_up_parts, down_parts)
    grad_packed = packed.transpose(1, 0, 2)
    qkv_rows = qkv_got[:, :128]
    out_sum = jnp.sum(out_got.astype(F32), axis=0).astype(BF16)
    qkv_full = both_cores(qkv_half)
    grad_input_attn = jnp.einsum(
        "tf,df->td", grad_packed.reshape(rows, 2048), qkv_full, preferred_element_type=F32
    )
    _, pull_attn_norm = jax.vjp(lambda v: rms_norm(v, attn_scale), x_in)
    (grad_in_norm,) = pull_attn_norm(grad_input_attn)
    input_grad = (grad_mid + grad_in_norm)[None]

    gain_got = jnp.sum(qkv_got[:, 128:].astype(F32), axis=0)
    gain_owned = jnp.stack(
        [
            gain_got[0, :128],
            gain_got[0, 128:],
            jnp.pad(gain_got[1, 0:8], (0, 120)),
            jnp.pad(gain_got[1, 8:16], (0, 120)),
        ]
    )
    gain_columns = jnp.pad(gain_owned.T, ((0, 0), (0, 252))).astype(BF16)

    own_half = lax.dynamic_update_slice(jnp.zeros((128, 1024), BF16), out_sum, (core * 64, 0))
    attn_rows = jnp.concatenate(
        [qkv_rows.reshape(8, 16, 8, 256).transpose(1, 0, 2, 3).reshape(16, 64, 256)]
        + [own_half[:, k * 256 : (k + 1) * 256].reshape(16, 8, 256) for k in range(4)]
        + [gain_columns.reshape(16, 8, 256)],
        axis=1,
    )
    rep_got, outputs = tie(lax.all_to_all(attn_rows, "rep", 0, 0), outputs)
    attn_part = jnp.sum(rep_got.astype(F32), axis=0).astype(BF16)
    attn_all = lax.all_to_all(
        jnp.broadcast_to(attn_part[None], (16, 104, 256)), "rep", 0, 0
    )
    heads_all = attn_all[:, :64].reshape(16, 8, 8, 256)

    def by_head(start, stop):
        width = stop - start
        cut = heads_all[:, :, :, start:stop].transpose(0, 2, 1, 3)
        return cut.reshape(128, 8 * width).astype(F32)

    out_all = jnp.concatenate(
        [attn_all[:, 64 + 8 * k : 72 + 8 * k].reshape(128, 256) for k in range(4)], axis=1
    ).astype(F32)
    gain_all = attn_all[:, 96:104].reshape(128, 256).astype(F32)

    gate_up_mine = jnp.stack(gate_up_parts)
    down_mine = jnp.stack(down_parts)
    gate_all, up_all, down_all = spread_slices(
        jnp.concatenate(
            [jnp.array([0, 2, 3, 1], jnp.int32)[(jnp.arange(4) - xpos) % 4], core[None]]
        ),
        gate_up_mine,
        send(gate_up_mine, CORE_SWAP),
        down_mine,
        send(down_mine, CORE_SWAP),
    )
    return (
        outputs,
        input_grad,
        by_head(0, 128),
        by_head(128, 192),
        by_head(192, 256),
        out_all,
        gate_all,
        up_all,
        down_all,
        gain_all[:, 0],
        gain_all[:, 1],
        gain_all[:8, 2],
        gain_all[:8, 3],
    )


def solution(mesh):
    shard = P("grp", None)
    return jax.shard_map(
        per_device,
        mesh=mesh,
        in_specs=(P("rep", "grp", None), P("rep", None))
        + (shard,) * 7
        + (P("grp"),) * 4
        + (P("rep", "grp", None),),
        out_specs=(P("rep", "grp", None),) * 2 + (shard,) * 7 + (P("grp"),) * 4,
        check_vma=False,
    )
```

```python
import functools
import math

import jax
import jax.numpy as jnp
from jax import lax
from jax.experimental import pallas as pl
from jax.experimental.pallas import tpu as pltpu
from jax.sharding import PartitionSpec as P

H = 16
KVH = 8
HD = 64
CH = 96
SEQ = 1536
SPANS = 16
TILE = 256
TILES = SEQ // TILE
EPS = 1e-05
THETA = 1000000.0
AXES = ("rep", "grp")
F32 = jnp.float32
BF16 = jnp.bfloat16
VMEM_LIMIT = 48 * 1024 * 1024


def coords(i):
    rep, grp = divmod(i, 8)
    return rep // 4, (rep // 2) % 2, rep % 2, grp // 4, grp % 4


def index_of(x, ylo, core, yhi, z):
    return ((x * 2 + ylo) * 2 + core) * 8 + yhi * 4 + z


def permutation(move):
    return [(i, index_of(*move(*coords(i)))) for i in range(128)]


X_UP = permutation(lambda x, a, c, b, z: ((x + 1) % 4, a, c, b, z))
X_DOWN = permutation(lambda x, a, c, b, z: ((x - 1) % 4, a, c, b, z))
Y_SWAP = permutation(lambda x, a, c, b, z: (x, 1 - a, c, b, z))
CORE_SWAP = permutation(lambda x, a, c, b, z: (x, a, 1 - c, b, z))


def send(value, perm):
    return lax.ppermute(value, AXES, perm)


def exchange_grp(value):
    return lax.all_to_all(value, "grp", 0, 0)


def to_grp(piece):
    return jnp.broadcast_to(piece[None], (8,) + piece.shape)


def x_gather(own):
    half = own.shape[0] // 2
    left = send(own, X_UP)
    right = send(own, X_DOWN)
    far_a = send(left[:half], X_UP)
    far_b = send(right[half:], X_DOWN)
    return own, left, right, jnp.concatenate([far_a, far_b], axis=0)


def x_reduce(parts):
    own, left, right, far = parts
    half = own.shape[0] // 2
    far = far.astype(BF16)
    got_a = send(far[:half], X_UP)
    got_b = send(far[half:], X_DOWN)
    right = jnp.concatenate([right[:half] + got_a.astype(F32), right[half:]], axis=0)
    left = jnp.concatenate([left[:half], left[half:] + got_b.astype(F32)], axis=0)
    from_left = send(right.astype(BF16), X_UP)
    from_right = send(left.astype(BF16), X_DOWN)
    return own + from_left.astype(F32) + from_right.astype(F32)


def tie(*values):
    return lax.optimization_barrier(values)


def rms_norm(values, gain):
    return values * lax.rsqrt(jnp.mean(values * values, axis=-1, keepdims=True) + EPS) * gain


def rotary():
    ladder = jnp.arange(HD // 2, dtype=F32) * (2.0 / HD)
    freq = jnp.exp(-math.log(THETA) * ladder)
    angle = jnp.arange(SEQ, dtype=F32)[None, :] * freq[:, None]
    return jnp.cos(angle), jnp.sin(angle)


def mask_tile():
    key = lax.broadcasted_iota(jnp.int32, (TILE, 2 * TILE), 0)
    query = lax.broadcasted_iota(jnp.int32, (TILE, 2 * TILE), 1)
    return key <= jnp.where(query >= TILE, query - TILE, query)


def dot(a, b):
    return jnp.dot(a, b, preferred_element_type=F32)


def span_of(i):
    return slice(i * TILE, (i + 1) * TILE)


def block_start(order_ref, c):
    return pl.multiple_of(order_ref[c] * CH, CH)


def forward_kernel(
    order_ref, tokens_ref, weight_ref, attn_gain_ref, head_gain_ref, cos_ref, sin_ref,
    mixed_ref, input_ref, cols_ref, rows_ref, lin_t_ref, out_t_ref, log_ref,
    lin_rows, keys, mixed_rows,
):
    for j in range(4):
        part = slice(j * 4 * CH, (j + 1) * 4 * CH)
        x = tokens_ref[part, :].astype(F32)
        r = lax.rsqrt(jnp.mean(x * x, axis=1, keepdims=True) + EPS)
        normed = (x * r * attn_gain_ref[...]).astype(BF16)
        input_ref[part, :] = normed
        lin = dot(normed, weight_ref[...])
        for k in range(4):
            lin_rows[pl.ds(block_start(order_ref, 4 * j + k), CH), :] = lin[k * CH : (k + 1) * CH, :]
    for i in range(TILES):
        span = span_of(i)
        lin_t = lin_rows[span, :].T
        lin_t_ref[:, span] = lin_t[0:192, :]
        cosine, sine = cos_ref[:, span], sin_ref[:, span]
        parts = []
        for h, kind, scale in ((0, 0, HD ** (-0.5)), (1, 0, HD ** (-0.5)), (2, 1, 1.0)):
            u = lin_t[h * 64 : (h + 1) * 64, :]
            r = lax.rsqrt(jnp.mean(u * u, axis=0, keepdims=True) + EPS)
            n = u * r * head_gain_ref[:, kind : kind + 1]
            low, high = n[:32, :], n[32:, :]
            parts += [(low * cosine - high * sine) * scale, (high * cosine + low * sine) * scale]
        both = jnp.concatenate(parts + [lin_t[192:256, :]], axis=0)
        cols_ref[:, span] = both.astype(BF16)
        flat = both.T.astype(BF16)
        rows_ref[span, :] = flat
        keys[span, :] = flat[:, 128:192]
    mask = mask_tile()
    for i in range(TILES):
        span = span_of(i)
        query = jnp.concatenate([cols_ref[0:64, span], cols_ref[64:128, span]], axis=1)
        total = jnp.zeros((64, 2 * TILE), F32)
        weight = jnp.zeros((1, 2 * TILE), F32)
        for c in range(i + 1):
            key_span = span_of(c)
            expo = jnp.exp(dot(keys[key_span, :], query))
            if c == i:
                expo = jnp.where(mask, expo, 0.0)
            weight = weight + jnp.sum(expo, axis=0, keepdims=True)
            total = total + dot(cols_ref[192:256, key_span], expo.astype(BF16))
        total = total / weight
        logs = jnp.log(weight)
        out_t_ref[0:64, span] = total[:, :TILE]
        out_t_ref[64:128, span] = total[:, TILE:]
        log_ref[0:1, span] = logs[:, :TILE]
        log_ref[1:2, span] = logs[:, TILE:]
        mixed_rows[span, :] = (
            jnp.concatenate([total[:, :TILE], total[:, TILE:]], axis=0).T.astype(BF16)
        )
    log_ref[2:8, :] = jnp.zeros((6, SEQ), F32)
    for c in range(SPANS):
        mixed_ref[c * CH : (c + 1) * CH, :] = mixed_rows[pl.ds(block_start(order_ref, c), CH), :]


VMEM_SPEC = pl.BlockSpec(memory_space=pltpu.VMEM)
SMEM_SPEC = pl.BlockSpec(memory_space=pltpu.SMEM)


def attend_forward(order, tokens, weight, attn_gain, head_gain, cosine, sine):
    return pl.pallas_call(
        forward_kernel,
        out_shape=(
            jax.ShapeDtypeStruct((SEQ, 128), BF16),
            jax.ShapeDtypeStruct((SEQ, 1024), BF16),
            jax.ShapeDtypeStruct((256, SEQ), BF16),
            jax.ShapeDtypeStruct((SEQ, 256), BF16),
            jax.ShapeDtypeStruct((192, SEQ), F32),
            jax.ShapeDtypeStruct((128, SEQ), F32),
            jax.ShapeDtypeStruct((8, SEQ), F32),
        ),
        in_specs=[SMEM_SPEC] + [VMEM_SPEC] * 6,
        out_specs=(VMEM_SPEC,) * 7,
        scratch_shapes=[
            pltpu.VMEM((SEQ, 256), F32),
            pltpu.VMEM((SEQ, 64), BF16),
            pltpu.VMEM((SEQ, 128), BF16),
        ],
        compiler_params=pltpu.CompilerParams(vmem_limit_bytes=VMEM_LIMIT),
        cost_estimate=pl.CostEstimate(
            flops=6 * 10**9, bytes_accessed=14 * 10**6, transcendentals=3 * 10**6
        ),
        name="attend_forward",
    )(order, tokens, weight, attn_gain, head_gain, cosine, sine)


def backward_kernel(
    order_ref, cols_ref, rows_ref, grad_ref, out_t_ref, log_ref, lin_t_ref, head_gain_ref,
    cos_ref, sin_ref, result_ref, gain_ref,
    grad_rows, grad_cols, keys, values, grad_keys, grad_values, grad_query, result_rows,
):
    for c in range(SPANS):
        grad_rows[pl.ds(block_start(order_ref, c), CH), :] = grad_ref[c * CH : (c + 1) * CH, :]
    for i in range(TILES):
        span = span_of(i)
        grad_cols[:, span] = grad_rows[span, :].astype(F32).T.astype(BF16)
        keys[span, :] = rows_ref[span, 128:192]
        values[span, :] = rows_ref[span, 192:256]
    grad_keys[...] = jnp.zeros_like(grad_keys)
    grad_values[...] = jnp.zeros_like(grad_values)
    mask = mask_tile()
    scale = HD ** (-0.5)
    for i in range(TILES):
        span = span_of(i)
        query = jnp.concatenate([cols_ref[0:64, span], cols_ref[64:128, span]], axis=1)
        grad = jnp.concatenate([grad_cols[0:64, span], grad_cols[64:128, span]], axis=1)
        query_rows = jnp.concatenate([rows_ref[span, 0:64], rows_ref[span, 64:128]], axis=0)
        grad_tile = jnp.concatenate([grad_rows[span, 0:64], grad_rows[span, 64:128]], axis=0)
        logs = jnp.concatenate([log_ref[0:1, span], log_ref[1:2, span]], axis=1)
        out_t = jnp.concatenate([out_t_ref[0:64, span], out_t_ref[64:128, span]], axis=1)
        inner = jnp.sum(out_t * grad.astype(F32), axis=0, keepdims=True)
        total = jnp.zeros((64, 2 * TILE), F32)
        for c in range(i + 1):
            key_span = span_of(c)
            attend = jnp.exp(dot(keys[key_span, :], query) - logs)
            if c == i:
                attend = jnp.where(mask, attend, 0.0)
            grad_values[key_span, :] += dot(attend.astype(BF16), grad_tile)
            grad_attend = dot(values[key_span, :], grad)
            grad_scores = (attend * (grad_attend - inner)).astype(BF16)
            grad_keys[key_span, :] += dot(grad_scores, query_rows)
            total = total + dot(cols_ref[128:192, key_span], grad_scores)
        total = total * scale
        grad_query[0:64, span] = total[:, :TILE]
        grad_query[64:128, span] = total[:, TILE:]
    sums = [jnp.zeros((64, TILE), F32), jnp.zeros((64, TILE), F32)]
    for i in range(TILES):
        span = span_of(i)
        cosine, sine = cos_ref[:, span], sin_ref[:, span]
        grads = (grad_query[0:64, span], grad_query[64:128, span], grad_keys[span, :].T)
        parts = []
        for h, kind in ((0, 0), (1, 0), (2, 1)):
            low, high = grads[h][:32, :], grads[h][32:, :]
            g = jnp.concatenate([low * cosine + high * sine, high * cosine - low * sine], axis=0)
            u = lin_t_ref[h * 64 : (h + 1) * 64, span]
            r = lax.rsqrt(jnp.mean(u * u, axis=0, keepdims=True) + EPS)
            wg = g * head_gain_ref[:, kind : kind + 1]
            mean = jnp.mean(u * wg, axis=0, keepdims=True)
            parts.append(wg * r - u * (r * r * r * mean))
            sums[kind] = sums[kind] + g * u * r
        flat = jnp.concatenate(parts, axis=0).T
        result_rows[span, :] = jnp.concatenate([flat, grad_values[span, :]], axis=1).astype(BF16)
    for kind in range(2):
        gain_ref[:, kind * 128 : (kind + 1) * 128] = jnp.broadcast_to(
            jnp.sum(sums[kind], axis=1, keepdims=True), (64, 128)
        )
    for c in range(SPANS):
        result_ref[c * CH : (c + 1) * CH, :] = result_rows[pl.ds(block_start(order_ref, c), CH), :]


def attend_backward(order, cols, rows, grad, out_t, logs, lin_t, head_gain, cosine, sine):
    return pl.pallas_call(
        backward_kernel,
        out_shape=(
            jax.ShapeDtypeStruct((SEQ, 256), BF16),
            jax.ShapeDtypeStruct((64, 256), F32),
        ),
        in_specs=[SMEM_SPEC] + [VMEM_SPEC] * 9,
        out_specs=(VMEM_SPEC,) * 2,
        scratch_shapes=[
            pltpu.VMEM((SEQ, 128), BF16),
            pltpu.VMEM((128, SEQ), BF16),
            pltpu.VMEM((SEQ, 64), BF16),
            pltpu.VMEM((SEQ, 64), BF16),
            pltpu.VMEM((SEQ, 64), F32),
            pltpu.VMEM((SEQ, 64), F32),
            pltpu.VMEM((128, SEQ), F32),
            pltpu.VMEM((SEQ, 256), BF16),
        ],
        compiler_params=pltpu.CompilerParams(vmem_limit_bytes=VMEM_LIMIT),
        cost_estimate=pl.CostEstimate(
            flops=10 * 10**9, bytes_accessed=8 * 10**6, transcendentals=3 * 10**6
        ),
        name="attend_backward",
    )(order, cols, rows, grad, out_t, logs, lin_t, head_gain, cosine, sine)


def spread_kernel(index_ref, mine_ref, other_ref, down_mine_ref, down_other_ref, gate_ref, up_ref, down_ref):
    core = index_ref[4]
    for x in range(4):
        for source, down_source, place in (
            (mine_ref, down_mine_ref, core),
            (other_ref, down_other_ref, 1 - core),
        ):
            block = source[index_ref[x]].astype(F32)
            rows = pl.ds(pl.multiple_of(place * 64, 64), 64)
            for k, target in enumerate((gate_ref, up_ref)):
                for g in range(8):
                    start = g * 576 + x * 144
                    target[rows, start : start + 144] = block[
                        :, k * 1152 + g * 144 : k * 1152 + (g + 1) * 144
                    ]
            down_rows = pl.ds(pl.multiple_of(x * 144 + place * 72, 8), 72)
            down_ref[down_rows, :] = down_source[index_ref[x]].astype(F32)


def spread_slices(index, mine, other, down_mine, down_other):
    return pl.pallas_call(
        spread_kernel,
        out_shape=(
            jax.ShapeDtypeStruct((128, 4608), F32),
            jax.ShapeDtypeStruct((128, 4608), F32),
            jax.ShapeDtypeStruct((576, 1024), F32),
        ),
        in_specs=[SMEM_SPEC] + [VMEM_SPEC] * 4,
        out_specs=(VMEM_SPEC,) * 3,
        compiler_params=pltpu.CompilerParams(vmem_limit_bytes=VMEM_LIMIT),
        cost_estimate=pl.CostEstimate(flops=10**7, bytes_accessed=10**7, transcendentals=0),
        name="spread_slices",
    )(index, mine, other, down_mine, down_other)


def swiglu(gate_in, up_in):
    return jax.nn.silu(gate_in) * up_in


def per_device(
    tokens, span_order, query_weight, key_weight, value_weight, out_weight,
    gate_weight, up_weight, down_weight, attn_gain, ffn_gain, query_gain, key_gain, cotangent,
):
    rep = lax.axis_index("rep")
    place = lax.axis_index("grp")
    xpos, core = rep // 4, rep % 2
    rows = tokens.shape[1]
    order_row = span_order[0]

    def core_half(matrix):
        half = matrix.shape[0] // 2
        return lax.dynamic_slice_in_dim(matrix, core * half, half, 0)

    def both_cores(mine):
        other = send(mine, CORE_SWAP)
        picked = lax.broadcasted_iota(jnp.int32, (1, 2, 1, 1), 1) == core
        return jnp.where(picked, mine[:, None], other[:, None]).reshape(-1, mine.shape[-1])

    grouped = jnp.concatenate(
        [
            query_weight.reshape(128, KVH, 128),
            key_weight.reshape(128, KVH, HD),
            value_weight.reshape(128, KVH, HD),
        ],
        axis=2,
    )
    gain_rows = jnp.concatenate(
        [
            jnp.concatenate([attn_gain, ffn_gain])[None],
            jnp.concatenate([query_gain, key_gain, jnp.zeros((240,), BF16)])[None],
            jnp.zeros((14, 256), BF16),
        ],
        axis=0,
    )
    got = exchange_grp(
        jnp.concatenate(
            [grouped.transpose(1, 0, 2), jnp.broadcast_to(gain_rows[None], (8, 16, 256))], axis=1
        )
    )
    all_tokens = lax.all_gather(tokens[0], "grp", axis=0, tiled=True)
    def x_columns(matrix):
        cut = matrix.reshape(128, 8, 4, 144)
        return lax.dynamic_index_in_dim(cut, xpos, 2, keepdims=False).reshape(128, 1152)

    gate_up_piece = core_half(jnp.concatenate([x_columns(gate_weight), x_columns(up_weight)], axis=1))
    down_piece = core_half(
        lax.dynamic_index_in_dim(down_weight.reshape(4, 144, 1024), xpos, 0, keepdims=False)
    )
    out_sent, got = tie(to_grp(core_half(out_weight)), got)
    out_half_weight = exchange_grp(out_sent)
    gate_up_sent, down_sent, qkv_sent, out_half_weight = tie(
        to_grp(gate_up_piece),
        to_grp(down_piece),
        to_grp(core_half(grouped.reshape(128, 2048))),
        out_half_weight,
    )
    down_half = exchange_grp(down_sent)

    cot = jnp.concatenate(x_gather(cotangent[0]), axis=0)

    head_weight = got[:, :128].reshape(1024, 256)
    attn_scale = got[:, 128, :128].reshape(1024).astype(F32)
    ffn_scale = got[:, 128, 128:].reshape(1024).astype(F32)
    head_gain = jnp.stack(
        [got[:, 129, 0:8].reshape(HD), got[:, 129, 8:16].reshape(HD)], axis=1
    ).astype(F32)
    x_in = tokens[0].astype(F32)
    cosine, sine = rotary()
    mixed_heads, input_attn, cols, rows_sorted, lin_t, out_t, logs = attend_forward(
        order_row, all_tokens, head_weight, attn_scale[None], head_gain, cosine, sine
    )
    mixed_heads, out_full, cot, down_half = tie(
        mixed_heads, both_cores(out_half_weight), cot, down_half
    )
    mixed = exchange_grp(mixed_heads.reshape(8, rows, 128))
    mixed, gate_up_sent = tie(mixed, gate_up_sent)
    gate_up_half = exchange_grp(gate_up_sent)
    mixed = mixed.transpose(1, 0, 2).reshape(rows, 1024)
    x_mid = x_in + dot(mixed, out_full)

    input_ffn_own = rms_norm(x_mid, ffn_scale).astype(BF16)
    input_ffn = jnp.concatenate(x_gather(input_ffn_own), axis=0)
    qkv_sent, gate_up_half, input_ffn, down_full = tie(
        qkv_sent, gate_up_half, input_ffn, both_cores(down_half)
    )
    qkv_half = exchange_grp(qkv_sent)
    gate_up_full = both_cores(gate_up_half)

    def core_sum(full, half):
        low = full.astype(BF16).reshape(8, 2, half, full.shape[-1])
        mine = lax.dynamic_index_in_dim(low, core, 1, keepdims=False)
        theirs = lax.dynamic_index_in_dim(low, 1 - core, 1, keepdims=False)
        return (mine.astype(F32) + send(theirs, CORE_SWAP).astype(F32)).astype(BF16)

    def y_sum(value):
        return (value.astype(F32) + send(value, Y_SWAP).astype(F32)).astype(BF16)

    def total(value):
        return jnp.sum(value.astype(F32), axis=0).astype(BF16)

    gate_up = dot(input_ffn, gate_up_full)
    gate, up_value = gate_up[:, :1152], gate_up[:, 1152:]
    hidden_exact, pull_swiglu = jax.vjp(swiglu, gate, up_value)
    hidden = hidden_exact.astype(BF16)
    down_grad = jnp.einsum("tf,td->fd", hidden, cot, preferred_element_type=F32)
    down_sent = core_sum(down_grad, 72)
    grad_hidden = jnp.einsum("td,fd->tf", cot, down_full, preferred_element_type=F32)
    grad_gate, grad_up = pull_swiglu(grad_hidden)
    grad_gate_up = jnp.concatenate([grad_gate.astype(BF16), grad_up.astype(BF16)], axis=1)
    grad_gate_up, down_sent, qkv_half = tie(grad_gate_up, down_sent, qkv_half)
    down_got = exchange_grp(down_sent)
    gate_up_grad = jnp.einsum("td,tf->df", input_ffn, grad_gate_up, preferred_element_type=F32)
    gate_up_sent = core_sum(gate_up_grad, 64)
    grad_input_part = jnp.einsum(
        "tf,df->td", grad_gate_up, gate_up_full, preferred_element_type=F32
    )
    grad_input_part, gate_up_sent, down_got = tie(grad_input_part, gate_up_sent, down_got)
    gate_up_got = exchange_grp(gate_up_sent)
    grad_input_ffn = x_reduce(grad_input_part.reshape(4, rows, 1024))
    grad_input_ffn, gate_up_got, down_sum, down_part = tie(
        grad_input_ffn, gate_up_got, total(down_got), dot(hidden, down_full)
    )

    _, pull_ffn_norm = jax.vjp(rms_norm, x_mid, ffn_scale)
    grad_mid_norm, ffn_gain_grad = pull_ffn_norm(grad_input_ffn)
    grad_mid = cotangent[0].astype(F32) + grad_mid_norm
    grad_attn = grad_mid.astype(BF16)
    grad_mixed = jnp.einsum(
        "td,fd->tf", grad_attn, out_full, preferred_element_type=F32
    ).astype(BF16)
    grad_sent, grad_attn, gate_up_got = tie(
        grad_mixed.reshape(rows, 8, 128).transpose(1, 0, 2), grad_attn, gate_up_got
    )
    grad_heads = exchange_grp(grad_sent)
    out_grad = jnp.einsum("tf,td->fd", mixed, grad_attn, preferred_element_type=F32)
    gate_up_sum = y_sum(total(gate_up_got))
    down_sum = y_sum(down_sum)
    out_sent = core_sum(out_grad, 64)
    grad_heads, out_sent, gate_up_sum, down_sum = tie(
        grad_heads, out_sent, gate_up_sum, down_sum
    )
    out_got = exchange_grp(out_sent)
    gate_up_parts = x_gather(gate_up_sum)
    down_parts = x_gather(down_sum)
    grad_lin, head_gain_grad = attend_backward(
        order_row, cols, rows_sorted, grad_heads.reshape(SEQ, 128), out_t, logs, lin_t,
        head_gain, cosine, sine,
    )
    qkv_grad = jnp.einsum("td,tf->df", input_attn, grad_lin, preferred_element_type=F32)
    grad_lin, out_got, down_part = tie(grad_lin, out_got, down_part)
    outputs = (x_mid + x_reduce(down_part.reshape(4, rows, 1024))).astype(BF16)[None]
    attn_gain_part = jnp.sum(qkv_grad * head_weight.astype(F32), axis=1) / attn_scale
    gain_parts = jnp.concatenate(
        [
            jnp.concatenate(
                [attn_gain_part.reshape(8, 1, 128), ffn_gain_grad.reshape(8, 1, 128)], axis=2
            ),
            jnp.concatenate(
                [
                    head_gain_grad[:, 0].reshape(8, 1, 8),
                    head_gain_grad[:, 128].reshape(8, 1, 8),
                    jnp.zeros((8, 1, 240), F32),
                ],
                axis=2,
            ),
            jnp.zeros((8, 14, 256), F32),
        ],
        axis=1,
    )
    packed = exchange_grp(grad_lin.reshape(8, rows, 256))
    qkv_sent = jnp.concatenate(
        [qkv_grad.astype(BF16).reshape(8, 128, 256), gain_parts.astype(BF16)], axis=1
    )
    qkv_sent, packed, qkv_half = tie(qkv_sent, packed, qkv_half)
    qkv_got = exchange_grp(qkv_sent)
    grad_packed = packed.transpose(1, 0, 2)
    qkv_rows = qkv_got[:, :128]
    out_sum = jnp.sum(out_got.astype(F32), axis=0).astype(BF16)
    qkv_full = both_cores(qkv_half)
    grad_input_attn = jnp.einsum(
        "tf,df->td", grad_packed.reshape(rows, 2048), qkv_full, preferred_element_type=F32
    )
    _, pull_attn_norm = jax.vjp(lambda v: rms_norm(v, attn_scale), x_in)
    (grad_in_norm,) = pull_attn_norm(grad_input_attn)
    input_grad = (grad_mid + grad_in_norm)[None]

    gain_got = jnp.sum(qkv_got[:, 128:].astype(F32), axis=0)
    gain_owned = jnp.stack(
        [
            gain_got[0, :128],
            gain_got[0, 128:],
            jnp.pad(gain_got[1, 0:8], (0, 120)),
            jnp.pad(gain_got[1, 8:16], (0, 120)),
        ]
    )
    gain_columns = jnp.pad(gain_owned.T, ((0, 0), (0, 252))).astype(BF16)

    own_half = lax.dynamic_update_slice(jnp.zeros((128, 1024), BF16), out_sum, (core * 64, 0))
    attn_rows = jnp.concatenate(
        [qkv_rows.reshape(8, 16, 8, 256).transpose(1, 0, 2, 3).reshape(16, 64, 256)]
        + [own_half[:, k * 256 : (k + 1) * 256].reshape(16, 8, 256) for k in range(4)]
        + [gain_columns.reshape(16, 8, 256)],
        axis=1,
    )
    rep_got, outputs, gate_up_parts, down_parts = tie(
        lax.all_to_all(attn_rows, "rep", 0, 0), outputs, gate_up_parts, down_parts
    )
    attn_part = jnp.sum(rep_got.astype(F32), axis=0).astype(BF16)
    attn_all = lax.all_to_all(
        jnp.broadcast_to(attn_part[None], (16, 104, 256)), "rep", 0, 0
    )
    heads_all = attn_all[:, :64].reshape(16, 8, 8, 256)

    def by_head(start, stop):
        width = stop - start
        cut = heads_all[:, :, :, start:stop].transpose(0, 2, 1, 3)
        return cut.reshape(128, 8 * width).astype(F32)

    out_all = jnp.concatenate(
        [attn_all[:, 64 + 8 * k : 72 + 8 * k].reshape(128, 256) for k in range(4)], axis=1
    ).astype(F32)
    gain_all = attn_all[:, 96:104].reshape(128, 256).astype(F32)

    gate_up_mine = jnp.stack(gate_up_parts)
    down_mine = jnp.stack(down_parts)
    gate_all, up_all, down_all = spread_slices(
        jnp.concatenate(
            [jnp.array([0, 2, 3, 1], jnp.int32)[(jnp.arange(4) - xpos) % 4], core[None]]
        ),
        gate_up_mine,
        send(gate_up_mine, CORE_SWAP),
        down_mine,
        send(down_mine, CORE_SWAP),
    )
    return (
        outputs,
        input_grad,
        by_head(0, 128),
        by_head(128, 192),
        by_head(192, 256),
        out_all,
        gate_all,
        up_all,
        down_all,
        gain_all[:, 0],
        gain_all[:, 1],
        gain_all[:8, 2],
        gain_all[:8, 3],
    )


def solution(mesh):
    shard = P("grp", None)
    return jax.shard_map(
        per_device,
        mesh=mesh,
        in_specs=(P("rep", "grp", None), P("rep", None))
        + (shard,) * 7
        + (P("grp"),) * 4
        + (P("rep", "grp", None),),
        out_specs=(P("rep", "grp", None),) * 2 + (shard,) * 7 + (P("grp"),) * 4,
        check_vma=False,
    )
```
